256 devices in a mesh: ctx: 32 (over y, x, core), tp: 8 (over z).
Axes of the slice: x: 4, y: 4, z: 8, core: 2. Of those that a mesh axis runs over, the one named last changes fastest.
Arguments:
- slow_x: bfloat16 [16384, 1024], P(('ctx', 'tp')), may hold values from -24 to 24
- q_weight: bfloat16 [1024, 1024], P(None, 'tp'), may hold values from -0.1875 to 0.1875
- o_weight: bfloat16 [1024, 1024], P('tp'), may hold values from -0.1875 to 0.1875
- fast_kv: bfloat16 [2, 131072, 1024], P(None, 'ctx', 'tp'), may hold values from -26 to 26
- mask_lists: int32 [128, 32], replicated, may hold values from 0 to 1023, as said below
- cotangent: bfloat16 [16384, 1024], P(('ctx', 'tp')), may hold values from -6 to 6
Outputs:
- attended: bfloat16 [16384, 1024], P(('ctx', 'tp'))
- grad_slow: bfloat16 [16384, 1024], P(('ctx', 'tp'))
- grad_q_weight: float32 [1024, 1024], P(None, 'tp')
- grad_o_weight: float32 [1024, 1024], P('tp')
- grad_kv: bfloat16 [2, 131072, 1024], P(None, 'ctx', 'tp')
The draws below stay inside these ranges and needn't reach their ends.
Inputs may be any that keep to these rules, and one draw needn't show every extreme that they name: `mask_lists`: row b lists the key blocks c - w to c + w - 1 that lie within the clip, where c = (2 b + 1) * 4 and w, drawn for each row, lies between 8 and 16; the remaining entries repeat c.
All inputs are finite; a program needn't handle non-finite values.
Results may differ from the reference program's by a relative error of at most 0.03.
Values may be sent and summed in bfloat16 or wider, within the bound.
No kernel may reach another device: no remote copies, remote signals or barrier semaphores. Data moves between devices by JAX's collectives and lax.ppermute only.
A program may use at most 128 MiB of HBM per device.

```python
import jax
import jax.numpy as jnp
from jax import lax

BLK = 128
REACH = 16
FAST_RATIO = 8
D = 1024
H = 16
DH = 64
S = 16384
F = 131072
NQB = 128
NFB = 1024


def draw_slow_x(key, part):
    key = jax.random.fold_in(key, 11)
    key_noise = jax.random.fold_in(key, 0)
    normal_draw = jnp.clip(jax.random.normal(key_noise, (S, D), jnp.float32), -6.0, 6.0)
    return normal_draw.astype(jnp.bfloat16)


def draw_fast_kv(key, part):
    key = jax.random.fold_in(key, 23)
    key_first = jax.random.fold_in(key, 0)
    key_value = jax.random.fold_in(key, 3)
    value_draw = jnp.clip(jax.random.normal(key_value, (F, D), jnp.float32), -6.0, 6.0)
    key_draw = jnp.clip(jax.random.normal(key_first, (F, D), jnp.float32), -6.0, 6.0)
    return jnp.stack([key_draw, value_draw]).astype(jnp.bfloat16)


def draw_mask_lists(key, part):
    key = jax.random.fold_in(key, 37)
    block_index = jnp.arange(NQB, dtype=jnp.int32)
    half_step = FAST_RATIO // 2
    centre = (2 * block_index + 1) * half_step
    band_width = jax.random.randint(key, (NQB,), REACH // 2, REACH + 1)
    offsets = jnp.arange(2 * REACH, dtype=jnp.int32) - REACH
    listed = centre[:, None] + offsets[None, :]
    inside = (offsets[None, :] >= -band_width[:, None]) & (offsets[None, :] < band_width[:, None])
    inside = inside & (listed >= 0) & (listed < NFB)
    return jnp.where(inside, listed, centre[:, None]).astype(jnp.int32)


def level_of(stream_key, extent, cuts, low, largest):
    loudness = 1.0
    for dim, parts in cuts:
        draws = jax.random.uniform(jax.random.fold_in(jax.random.fold_in(stream_key, 6), dim), (parts,), jnp.float32, low / len(cuts), largest / len(cuts))
        loudness = loudness * jnp.repeat(jnp.exp(draws), extent[dim] // parts).reshape((-1,) + (1,) * (len(extent) - 1 - dim))
    return loudness


def bell_draw(own_key, dims, spread, reach, cuts=(), held_as=jnp.bfloat16):
    entries = spread * jax.random.normal(own_key, dims, jnp.float32)
    if cuts:
        entries = entries * level_of(own_key, dims, cuts, -0.22, 0.18)
    return jnp.clip(entries, -reach, reach).astype(held_as)


def setup_inputs(seed: int = 0) -> dict:
    keys = jax.random.split(jax.random.key(seed), 7)
    slow_x = draw_slow_x(jax.random.fold_in(keys[6], 71), 0)
    q_weight = bell_draw(keys[1], (D, D), D ** -0.5, 0.1875, ((1, 8),))
    o_weight = bell_draw(keys[2], (D, D), D ** -0.5, 0.1875, ((0, 8),))
    fast_kv = draw_fast_kv(jax.random.fold_in(keys[6], 71), 0)
    mask_lists = draw_mask_lists(jax.random.fold_in(keys[6], 71), 0)
    cotangent = bell_draw(keys[5], (S, D), 1.0, 6.0, ((0, 256),))
    return {"slow_x": slow_x, "q_weight": q_weight, "o_weight": o_weight, "fast_kv": fast_kv, "mask_lists": mask_lists, "cotangent": cotangent}


def reference(slow_x, q_weight, o_weight, fast_kv, mask_lists, cotangent):
    score_scale = DH ** -0.5
    window_rows = 2 * REACH * BLK
    margin = REACH * BLK
    half_step = FAST_RATIO // 2
    queries = (jnp.dot(slow_x, q_weight, preferred_element_type=jnp.float32) * score_scale).astype(jnp.bfloat16)
    grad_attn = jnp.dot(cotangent, o_weight.T, preferred_element_type=jnp.float32).astype(jnp.bfloat16)
    key_rows = jnp.pad(fast_kv[0], ((margin, margin), (0, 0)))
    value_rows = jnp.pad(fast_kv[1], ((margin, margin), (0, 0)))
    offsets = jnp.arange(2 * REACH, dtype=jnp.int32) - REACH

    def one_block(carried, inputs):
        grad_keys, grad_values = carried
        block_index, query_block, grad_block, band_list = inputs
        centre = (2 * block_index + 1) * half_step
        start_row = (centre * BLK).astype(jnp.int32)
        key_win = lax.dynamic_slice_in_dim(key_rows, start_row, window_rows, 0).astype(jnp.float32).reshape(window_rows, H, DH)
        val_win = lax.dynamic_slice_in_dim(value_rows, start_row, window_rows, 0).astype(jnp.float32).reshape(window_rows, H, DH)
        wanted = centre + offsets
        allowed = jnp.any(band_list[:, None] == wanted[None, :], axis=0)
        live_keys = jnp.repeat(allowed, BLK)
        query_full = query_block.astype(jnp.float32).reshape(BLK, H, DH)
        grad_full = grad_block.astype(jnp.float32).reshape(BLK, H, DH)
        scores = jnp.einsum("qhd,khd->hqk", query_full, key_win)
        scores = jnp.where(live_keys[None, None, :], scores, -jnp.inf)
        row_max = jnp.max(scores, axis=-1, keepdims=True)
        log_total = row_max + jnp.log(jnp.sum(jnp.exp(scores - row_max), axis=-1, keepdims=True))
        prob_full = jnp.exp(scores - log_total)
        prob_half = prob_full.astype(jnp.bfloat16)
        attended_block = jnp.einsum("hqk,khd->qhd", prob_half.astype(jnp.float32), val_win).astype(jnp.bfloat16)
        row_delta = jnp.sum(grad_full * attended_block.astype(jnp.float32), axis=-1)
        grad_prob = jnp.einsum("qhd,khd->hqk", grad_full, val_win)
        grad_score = (prob_full * (grad_prob - row_delta.T[:, :, None])).astype(jnp.bfloat16)
        grad_query = jnp.einsum("hqk,khd->qhd", grad_score.astype(jnp.float32), key_win)
        grad_key = jnp.einsum("hqk,qhd->khd", grad_score.astype(jnp.float32), query_full).reshape(window_rows, D)
        grad_value = jnp.einsum("hqk,qhd->khd", prob_half.astype(jnp.float32), grad_full).reshape(window_rows, D)
        old_keys = lax.dynamic_slice_in_dim(grad_keys, start_row, window_rows, 0)
        grad_keys = lax.dynamic_update_slice_in_dim(grad_keys, old_keys + grad_key, start_row, 0)
        old_values = lax.dynamic_slice_in_dim(grad_values, start_row, window_rows, 0)
        grad_values = lax.dynamic_update_slice_in_dim(grad_values, old_values + grad_value, start_row, 0)
        grad_pre = (grad_query.reshape(BLK, D) * score_scale).astype(jnp.bfloat16)
        return (grad_keys, grad_values), (attended_block.reshape(BLK, D), grad_pre)

    zeros_rows = jnp.zeros(key_rows.shape, jnp.float32)
    inputs = (jnp.arange(NQB, dtype=jnp.int32), queries.reshape(NQB, BLK, D), grad_attn.reshape(NQB, BLK, D), mask_lists)
    (grad_keys, grad_values), (attn_blocks, grad_blocks) = lax.scan(one_block, (zeros_rows, zeros_rows), inputs)
    attn = attn_blocks.reshape(S, D)
    grad_pre = grad_blocks.reshape(S, D)
    attended = jnp.dot(attn, o_weight, preferred_element_type=jnp.float32).astype(jnp.bfloat16)
    grad_o_weight = jnp.dot(attn.T, cotangent, preferred_element_type=jnp.float32)
    grad_q_weight = jnp.dot(slow_x.T, grad_pre, preferred_element_type=jnp.float32)
    grad_slow = jnp.dot(grad_pre, q_weight.T, preferred_element_type=jnp.float32).astype(jnp.bfloat16)
    grad_kv = jnp.stack([grad_keys[margin:margin + F], grad_values[margin:margin + F]]).astype(jnp.bfloat16)
    return (attended, grad_slow, grad_q_weight, grad_o_weight, grad_kv)
```

```python
import functools

import jax
import jax.numpy as jnp
from jax import lax
from jax.experimental import pallas as pl
from jax.experimental.pallas import tpu as pltpu
from jax.sharding import PartitionSpec as P

BLK = 128
DH = 64
CHUNK = 512
MASKED = -1e30
VMEM_LIMIT = 56 * 1024 * 1024


def contract(a, b, dims):
    return lax.dot_general(a, b, (dims, ((), ())), preferred_element_type=jnp.float32)


def row_split(block):
    lane = lax.broadcasted_iota(jnp.int32, block.shape, 1)
    zero = jnp.zeros_like(block)
    return jnp.concatenate([jnp.where(lane < DH, block, zero), jnp.where(lane >= DH, block, zero)], axis=0)


def column_split(block):
    row = lax.broadcasted_iota(jnp.int32, block.shape, 0)
    zero = jnp.zeros_like(block)
    return jnp.concatenate([jnp.where(row < DH, block, zero), jnp.where(row >= DH, block, zero)], axis=1)


def column_join(wide):
    row = lax.broadcasted_iota(jnp.int32, (wide.shape[0], BLK), 0)
    return jnp.where(row < DH, wide[:, :BLK], wide[:, BLK:])


def load_extended(half, left, own, right, dest, sems):
    rim, rows = left.shape[1], own.shape[1]
    copies = [
        pltpu.make_async_copy(left.at[half], dest.at[pl.ds(0, rim)], sems.at[0]),
        pltpu.make_async_copy(own.at[half], dest.at[pl.ds(rim, rows)], sems.at[1]),
        pltpu.make_async_copy(right.at[half], dest.at[pl.ds(rim + rows, rim)], sems.at[2]),
    ]
    for copy in copies:
        copy.start()
    return copies


def transpose_into(source, dest):
    for first in range(0, source.shape[0], CHUNK):
        dest[:, first : first + CHUNK] = source[first : first + CHUNK, :].T


def forward_kernel(step_rows, window, bias, q, left, own, right, probs, attn, inverse,
                   keys, values, values_t, score, sems_k, sems_v):
    block = pl.program_id(0)

    @pl.when(block == 0)
    def _():
        first = load_extended(1, left, own, right, values, sems_v)
        second = load_extended(0, left, own, right, keys, sems_k)
        for copy in first:
            copy.wait()
        transpose_into(values, values_t)
        for copy in second:
            copy.wait()

    base = block * step_rows
    q_t = column_split(q[...].T)
    top = jnp.full((8, 2 * BLK), -jnp.inf, jnp.float32)
    for c in range(window // CHUNK):
        at = pl.multiple_of(base + c * CHUNK, CHUNK)
        s = contract(keys[pl.ds(at, CHUNK), :], q_t, ((1,), (0,)))
        for j in range(CHUNK // BLK):
            part = s[j * BLK : (j + 1) * BLK] + bias[block, c * (CHUNK // BLK) + j]
            score[c * CHUNK + j * BLK : c * CHUNK + (j + 1) * BLK, :] = part
            top = jnp.maximum(top, jnp.max(part.reshape(BLK // 8, 8, 2 * BLK), axis=0))
    row_max = jnp.max(top, axis=0, keepdims=True)
    total = jnp.zeros((8, 2 * BLK), jnp.float32)
    out = jnp.zeros((BLK, 2 * BLK), jnp.float32)
    for c in range(window // CHUNK):
        at = pl.multiple_of(base + c * CHUNK, CHUNK)
        e = jnp.exp(score[c * CHUNK : (c + 1) * CHUNK, :] - row_max)
        total = total + jnp.sum(e.reshape(CHUNK // 8, 8, 2 * BLK), axis=0)
        half = e.astype(jnp.bfloat16)
        probs[0, c * CHUNK : (c + 1) * CHUNK, :] = half
        out = out + contract(values_t[:, pl.ds(at, CHUNK)], half, ((1,), (0,)))
    inv = 1.0 / jnp.sum(total, axis=0, keepdims=True)
    attn[...] = column_join(out * inv).T.astype(jnp.bfloat16)
    inverse[0] = jnp.broadcast_to(inv, (8, 2 * BLK))


def backward_kernel(step_rows, window, scale, q, grad, attn, inverse, probs, left, own, right,
                    grad_pre, own_grads, left_grads, right_grads,
                    keys, values, keys_t, acc_k, acc_v, sems_k, sems_v):
    block = pl.program_id(0)
    rim, rows = left.shape[1], own.shape[1]
    kept = window - step_rows

    @pl.when(block == 0)
    def _():
        first = load_extended(0, left, own, right, keys, sems_k)
        second = load_extended(1, left, own, right, values, sems_v)
        acc_k[:kept, :] = jnp.zeros((kept, BLK), jnp.float32)
        acc_v[:kept, :] = jnp.zeros((kept, BLK), jnp.float32)
        for copy in first:
            copy.wait()
        transpose_into(keys, keys_t)
        for copy in second:
            copy.wait()

    base = block * step_rows
    inv = inverse[0, :1, :]
    grad_t = grad[...].astype(jnp.float32).T
    attn_t = attn[...].astype(jnp.float32).T
    product = grad_t * attn_t
    delta = jnp.concatenate(
        [jnp.sum(product[:DH], axis=0, keepdims=True), jnp.sum(product[DH:], axis=0, keepdims=True)], axis=1
    ) * inv
    scaled = column_split(grad_t) * inv
    grad_cols = scaled.astype(jnp.bfloat16)
    grad_rows = scaled.T.astype(jnp.bfloat16)
    query_rows = row_split(q[...])
    total = jnp.zeros((BLK, 2 * BLK), jnp.float32)
    for c in range(window // CHUNK):
        at = pl.multiple_of(base + c * CHUNK, CHUNK)
        e = probs[0, c * CHUNK : (c + 1) * CHUNK, :]
        dp = contract(values[pl.ds(at, CHUNK), :], grad_cols, ((1,), (0,)))
        ds = (e.astype(jnp.float32) * (dp - delta)).astype(jnp.bfloat16)
        total = total + contract(keys_t[:, pl.ds(at, CHUNK)], ds, ((1,), (0,)))
        gk = contract(ds, query_rows, ((1,), (0,)))
        gv = contract(e, grad_rows, ((1,), (0,)))
        if c * CHUNK < kept:
            gk = gk + acc_k[pl.ds(at, CHUNK), :]
            gv = gv + acc_v[pl.ds(at, CHUNK), :]
        acc_k[pl.ds(at, CHUNK), :] = gk
        acc_v[pl.ds(at, CHUNK), :] = gv
    grad_pre[...] = (column_join(total) * scale).T.astype(jnp.bfloat16)

    @pl.when(block == pl.num_programs(0) - 1)
    def _():
        for half, acc in ((0, acc_k), (1, acc_v)):
            left_grads[half] = acc[:rim, :].astype(jnp.bfloat16)
            right_grads[half] = acc[rim + rows :, :].astype(jnp.bfloat16)
            own_grads[half] = acc[rim : rim + rows, :]


def whole(shape):
    return pl.BlockSpec(shape, lambda i: (0,) * len(shape))


def attention_forward(bias, q, left, own, right, step_rows, window):
    blocks = q.shape[0] // BLK
    ext = left.shape[1] + own.shape[1] + right.shape[1]
    anywhere = pl.BlockSpec(memory_space=pl.ANY)
    return pl.pallas_call(
        functools.partial(forward_kernel, step_rows, window),
        grid=(blocks,),
        in_specs=[
            pl.BlockSpec(memory_space=pltpu.SMEM),
            pl.BlockSpec((BLK, BLK), lambda i: (i, 0)),
            anywhere, anywhere, anywhere,
        ],
        out_specs=[
            pl.BlockSpec((1, window, 2 * BLK), lambda i: (i, 0, 0)),
            pl.BlockSpec((BLK, BLK), lambda i: (i, 0)),
            pl.BlockSpec((1, 8, 2 * BLK), lambda i: (i, 0, 0)),
        ],
        out_shape=[
            jax.ShapeDtypeStruct((blocks, window, 2 * BLK), jnp.bfloat16),
            jax.ShapeDtypeStruct(q.shape, jnp.bfloat16),
            jax.ShapeDtypeStruct((blocks, 8, 2 * BLK), jnp.float32),
        ],
        scratch_shapes=[
            pltpu.VMEM((ext, BLK), jnp.bfloat16),
            pltpu.VMEM((ext, BLK), jnp.bfloat16),
            pltpu.VMEM((BLK, ext), jnp.bfloat16),
            pltpu.VMEM((window, 2 * BLK), jnp.float32),
            pltpu.SemaphoreType.DMA((3,)),
            pltpu.SemaphoreType.DMA((3,)),
        ],
        compiler_params=pltpu.CompilerParams(
            dimension_semantics=("arbitrary",), vmem_limit_bytes=VMEM_LIMIT
        ),
        cost_estimate=pl.CostEstimate(
            flops=blocks * 4 * window * BLK * BLK * 2, bytes_accessed=14_000_000,
            transcendentals=blocks * window * 2 * BLK,
        ),
        name="attention_forward",
    )(bias, q, left, own, right)


def attention_backward(q, grad, attn, inverse, probs, left, own, right, step_rows, window):
    blocks = q.shape[0] // BLK
    rim, rows = left.shape[1], own.shape[1]
    ext = rim + rows + rim
    anywhere = pl.BlockSpec(memory_space=pl.ANY)
    row_block = pl.BlockSpec((BLK, BLK), lambda i: (i, 0))
    return pl.pallas_call(
        functools.partial(backward_kernel, step_rows, window, DH ** -0.5),
        grid=(blocks,),
        in_specs=[
            row_block, row_block, row_block,
            pl.BlockSpec((1, 8, 2 * BLK), lambda i: (i, 0, 0)),
            pl.BlockSpec((1, window, 2 * BLK), lambda i: (i, 0, 0)),
            anywhere, anywhere, anywhere,
        ],
        out_specs=[row_block, whole((2, rows, BLK)), whole((2, rim, BLK)), whole((2, rim, BLK))],
        out_shape=[
            jax.ShapeDtypeStruct(q.shape, jnp.bfloat16),
            jax.ShapeDtypeStruct((2, rows, BLK), jnp.float32),
            jax.ShapeDtypeStruct((2, rim, BLK), jnp.bfloat16),
            jax.ShapeDtypeStruct((2, rim, BLK), jnp.bfloat16),
        ],
        scratch_shapes=[
            pltpu.VMEM((ext, BLK), jnp.bfloat16),
            pltpu.VMEM((ext, BLK), jnp.bfloat16),
            pltpu.VMEM((BLK, ext), jnp.bfloat16),
            pltpu.VMEM((ext, BLK), jnp.float32),
            pltpu.VMEM((ext, BLK), jnp.float32),
            pltpu.SemaphoreType.DMA((3,)),
            pltpu.SemaphoreType.DMA((3,)),
        ],
        compiler_params=pltpu.CompilerParams(
            dimension_semantics=("arbitrary",), vmem_limit_bytes=VMEM_LIMIT
        ),
        cost_estimate=pl.CostEstimate(
            flops=blocks * 8 * window * BLK * BLK * 2, bytes_accessed=20_000_000, transcendentals=0
        ),
        name="attention_backward",
    )(q, grad, attn, inverse, probs, left, own, right)


def shifted(count, by):
    return [(i, (i + by) % count) for i in range(count)]


def ring_gather(shard, axis):
    count = lax.axis_size(axis)
    here = lax.axis_index(axis)
    rows = shard.shape[0]
    pieces = [(shard, 0)]
    forward = backward = shard
    for step in range(1, count // 2 + 1):
        forward = lax.ppermute(forward, axis, shifted(count, 1))
        pieces.append((forward, -step))
        if step < count - step:
            backward = lax.ppermute(backward, axis, shifted(count, -1))
            pieces.append((backward, step))
    out = jnp.zeros((count * rows,) + shard.shape[1:], shard.dtype)
    for piece, by in pieces:
        out = lax.dynamic_update_slice_in_dim(out, piece, lax.rem(here + by + count, count) * rows, 0)
    return out


def band_bias(band_lists, base_block, query_blocks, half_step, reach_blocks):
    local = jnp.arange(query_blocks, dtype=jnp.int32)
    window_first = base_block + (2 * local + 1) * half_step - reach_blocks
    wanted = window_first[:, None] + jnp.arange(2 * reach_blocks, dtype=jnp.int32)[None, :]
    allowed = jnp.any(band_lists[:, :, None] == wanted[:, None, :], axis=1)
    return jnp.where(allowed, 0.0, MASKED).astype(jnp.float32)


def sum_everywhere(partial, axis):
    count = lax.axis_size(axis)
    shape = partial.shape
    parts = partial.astype(jnp.bfloat16).reshape(count, -1, BLK)
    arrived = lax.all_to_all(parts, axis, 0, 0, tiled=True)
    own = jnp.sum(arrived.astype(jnp.float32), axis=0, keepdims=True).astype(jnp.bfloat16)
    spread = lax.all_to_all(jnp.broadcast_to(own, parts.shape), axis, 0, 0, tiled=True)
    return spread.reshape(shape).astype(jnp.float32)


def on_device(slow_x, q_weight, o_weight, fast_kv, mask_lists, cotangent):
    own_rows, width = slow_x.shape
    tp = lax.axis_size("tp")
    ctx = lax.axis_size("ctx")
    total_rows = own_rows * tp
    query_blocks = total_rows // BLK
    fast_rows = fast_kv.shape[1]
    fast_blocks = fast_rows // BLK
    half_step = fast_blocks // (2 * query_blocks)
    reach_blocks = mask_lists.shape[1] // 2
    rim = (reach_blocks - half_step) * BLK
    window = 2 * reach_blocks * BLK
    step_rows = 2 * half_step * BLK
    scale = DH ** -0.5

    up = [(i, i + 1) for i in range(ctx - 1)]
    down = [(i + 1, i) for i in range(ctx - 1)]
    left = lax.ppermute(fast_kv[:, fast_rows - rim :], "ctx", up)
    right = lax.ppermute(fast_kv[:, :rim], "ctx", down)

    weights = lax.all_gather(jnp.concatenate([o_weight, q_weight.T], axis=1), "tp", axis=0, tiled=True)

    both = ring_gather(jnp.concatenate([slow_x, cotangent], axis=1), "tp")
    rows_x, rows_g = both[:, :width], both[:, width:]

    ctx_index = lax.axis_index("ctx")
    band_lists = lax.dynamic_slice_in_dim(mask_lists, ctx_index * query_blocks, query_blocks, 0)
    bias = band_bias(band_lists, ctx_index * fast_blocks, query_blocks, half_step, reach_blocks)

    queries = (contract(rows_x, q_weight, ((1,), (0,))) * scale).astype(jnp.bfloat16)
    grad_attn = contract(rows_g, o_weight, ((1,), (1,))).astype(jnp.bfloat16)

    probs, attn, inverse = attention_forward(bias, queries, left, fast_kv, right, step_rows, window)
    grad_pre, own_grads, left_grads, right_grads = attention_backward(
        queries, grad_attn, attn, inverse, probs, left, fast_kv, right, step_rows, window
    )

    from_right = lax.ppermute(left_grads, "ctx", down)
    from_left = lax.ppermute(right_grads, "ctx", up)
    own_grads = own_grads.at[:, :rim].add(from_left.astype(jnp.float32))
    own_grads = own_grads.at[:, fast_rows - rim :].add(from_right.astype(jnp.float32))
    grad_kv = own_grads.astype(jnp.bfloat16)

    query_term = contract(rows_x, grad_pre, ((0,), (0,)))
    output_term = contract(attn, rows_g, ((0,), (0,)))
    mixed = jnp.concatenate([attn, grad_pre], axis=1).reshape(tp, own_rows, 2 * BLK)
    mixed = lax.all_to_all(mixed, "tp", 0, 0, tiled=True)
    full = weights.reshape(tp, BLK, 2 * width)
    attended = jnp.einsum(
        "trk,tkn->rn", mixed[:, :, :BLK], full[:, :, :width], preferred_element_type=jnp.float32
    ).astype(jnp.bfloat16)
    grad_slow = jnp.einsum(
        "trk,tkn->rn", mixed[:, :, BLK:], full[:, :, width:], preferred_element_type=jnp.float32
    ).astype(jnp.bfloat16)

    terms = jnp.concatenate([query_term.reshape(-1, BLK), output_term.reshape(-1, BLK)], axis=0)
    terms = sum_everywhere(terms, "ctx")
    half = width * q_weight.shape[1] // BLK
    grad_q_weight = terms[:half].reshape(q_weight.shape)
    grad_o_weight = terms[half:].reshape(o_weight.shape)
    return (attended, grad_slow, grad_q_weight, grad_o_weight, grad_kv)


def solution(mesh):
    in_specs = (
        P(("ctx", "tp"), None),
        P(None, "tp"),
        P("tp", None),
        P(None, "ctx", "tp"),
        P(),
        P(("ctx", "tp"), None),
    )
    out_specs = (
        P(("ctx", "tp"), None),
        P(("ctx", "tp"), None),
        P(None, "tp"),
        P("tp", None),
        P(None, "ctx", "tp"),
    )
    return jax.shard_map(on_device, mesh=mesh, in_specs=in_specs, out_specs=out_specs, check_vma=False)
```

```python
import functools

import jax
import jax.numpy as jnp
from jax import lax
from jax.experimental import pallas as pl
from jax.experimental.pallas import tpu as pltpu
from jax.sharding import PartitionSpec as P

BLK = 128
DH = 64
CHUNK = 512
MASKED = -1e30
VMEM_LIMIT = 56 * 1024 * 1024


def contract(a, b, dims):
    return lax.dot_general(a, b, (dims, ((), ())), preferred_element_type=jnp.float32)


def row_split(block):
    lane = lax.broadcasted_iota(jnp.int32, block.shape, 1)
    zero = jnp.zeros_like(block)
    return jnp.concatenate([jnp.where(lane < DH, block, zero), jnp.where(lane >= DH, block, zero)], axis=0)


def column_split(block):
    row = lax.broadcasted_iota(jnp.int32, block.shape, 0)
    zero = jnp.zeros_like(block)
    return jnp.concatenate([jnp.where(row < DH, block, zero), jnp.where(row >= DH, block, zero)], axis=1)


def column_join(wide):
    row = lax.broadcasted_iota(jnp.int32, (wide.shape[0], BLK), 0)
    return jnp.where(row < DH, wide[:, :BLK], wide[:, BLK:])


def load_extended(half, left, own, right, dest, sems):
    rim, rows = left.shape[1], own.shape[1]
    copies = [
        pltpu.make_async_copy(left.at[half], dest.at[pl.ds(0, rim)], sems.at[0]),
        pltpu.make_async_copy(own.at[half], dest.at[pl.ds(rim, rows)], sems.at[1]),
        pltpu.make_async_copy(right.at[half], dest.at[pl.ds(rim + rows, rim)], sems.at[2]),
    ]
    for copy in copies:
        copy.start()
    return copies


def transpose_kernel(left, own, right, out):
    first = 0
    for piece in (left, own, right):
        rows = piece.shape[1]
        for row in range(0, rows, CHUNK):
            out[0, :, first + row : first + row + CHUNK] = piece[0, row : row + CHUNK, :].T
        first += rows


def forward_kernel(step_rows, window, scale, bias, x, weight, left, own, right, flipped,
                   probs, attn, factor, queries, keys, values_t, parts, sems_k, sem_v):
    block = pl.program_id(0)

    @pl.when(block == 0)
    def _():
        first = load_extended(0, left, own, right, keys, sems_k)
        second = pltpu.make_async_copy(flipped.at[1], values_t, sem_v)
        second.start()
        for copy in first:
            copy.wait()
        second.wait()

    base = block * step_rows
    chunks = window // CHUNK
    per = CHUNK // BLK
    q = (contract(x[...], weight[...], ((1,), (0,))) * scale).astype(jnp.bfloat16)
    queries[...] = q
    q_t = column_split(q.T)
    at = lambda c: pl.ds(pl.multiple_of(base + c * CHUNK, CHUNK), CHUNK)
    scores = lambda c: contract(keys[at(c), :], q_t, ((1,), (0,)))
    tops, sums = [], []
    ahead, held = scores(0), None

    def weigh(c, half):
        parts[c] = contract(values_t[:, at(c)], half, ((1,), (0,)))

    for c in range(chunks):
        s = ahead
        if c + 1 < chunks:
            ahead = scores(c + 1)
        s = jnp.concatenate([s[j * BLK : (j + 1) * BLK] + bias[block, c * per + j] for j in range(per)], axis=0)
        top = jnp.max(jnp.max(s.reshape(CHUNK // 8, 8, 2 * BLK), axis=0), axis=0, keepdims=True)
        e = jnp.exp(s - top)
        tops.append(top)
        sums.append(jnp.sum(jnp.sum(e.reshape(CHUNK // 8, 8, 2 * BLK), axis=0), axis=0, keepdims=True))
        half = e.astype(jnp.bfloat16)
        probs[0, c * CHUNK : (c + 1) * CHUNK, :] = half
        if held is not None:
            weigh(c - 1, held)
        held = half
    weigh(chunks - 1, held)
    tops = jnp.concatenate(tops, axis=0)
    sums = jnp.concatenate(sums, axis=0)
    f = jnp.exp(tops - jnp.max(tops, axis=0, keepdims=True))
    f = f * (1.0 / jnp.sum(f * sums, axis=0, keepdims=True))
    out = parts[0] * f[:1]
    for c in range(1, chunks):
        out = out + parts[c] * f[c : c + 1]
    attn[...] = column_join(out).T.astype(jnp.bfloat16)
    factor[0] = f


def backward_kernel(step_rows, window, scale, x, g, weight, queries, attn, factor, probs,
                    left, own, right, flipped,
                    grad_pre, own_grads, left_grads, right_grads, terms,
                    values, keys_t, acc_k, acc_v, acc_q, acc_o, sems_v, sem_k):
    block = pl.program_id(0)
    rim, rows = left.shape[1], own.shape[1]
    kept = window - step_rows
    chunks = window // CHUNK

    @pl.when(block == 0)
    def _():
        first = load_extended(1, left, own, right, values, sems_v)
        second = pltpu.make_async_copy(flipped.at[0], keys_t, sem_k)
        second.start()
        acc_k[:kept, :] = jnp.zeros((kept, BLK), jnp.float32)
        acc_v[:kept, :] = jnp.zeros((kept, BLK), jnp.float32)
        acc_q[...] = jnp.zeros(acc_q.shape, jnp.float32)
        acc_o[...] = jnp.zeros(acc_o.shape, jnp.float32)
        for copy in first:
            copy.wait()
        second.wait()

    base = block * step_rows
    at = lambda c: pl.ds(pl.multiple_of(base + c * CHUNK, CHUNK), CHUNK)
    grad = contract(g[...], weight[...], ((1,), (1,))).astype(jnp.bfloat16).astype(jnp.float32)
    grad_t = grad.T
    product = grad_t * attn[...].astype(jnp.float32).T
    delta = jnp.concatenate(
        [jnp.sum(product[:DH], axis=0, keepdims=True), jnp.sum(product[DH:], axis=0, keepdims=True)], axis=1
    )
    wide, tall = column_split(grad_t), row_split(grad)
    query_rows = row_split(queries[...])
    f = factor[0]
    f_t = f.T
    lift = lambda c: contract(values[at(c), :], (wide * f[c : c + 1]).astype(jnp.bfloat16), ((1,), (0,)))
    total = jnp.zeros((BLK, 2 * BLK), jnp.float32)
    ahead = lift(0)
    for c in range(chunks):
        dp = ahead
        if c + 1 < chunks:
            ahead = lift(c + 1)
        e = probs[0, c * CHUNK : (c + 1) * CHUNK, :]
        ds = (e.astype(jnp.float32) * (dp - delta * f[c : c + 1])).astype(jnp.bfloat16)
        total = total + contract(keys_t[:, at(c)], ds, ((1,), (0,)))
        gk = contract(ds, query_rows, ((1,), (0,)))
        gv = contract(e, (tall * f_t[:, c : c + 1]).astype(jnp.bfloat16), ((1,), (0,)))
        if c * CHUNK < kept:
            gk = gk + acc_k[at(c), :]
            gv = gv + acc_v[at(c), :]
        acc_k[at(c), :] = gk
        acc_v[at(c), :] = gv
    pre = (column_join(total) * scale).T.astype(jnp.bfloat16)
    grad_pre[...] = pre
    acc_q[...] += contract(x[...], pre, ((0,), (0,)))
    acc_o[...] += contract(g[...], attn[...], ((0,), (0,)))

    @pl.when(block == pl.num_programs(0) - 1)
    def _():
        for half, acc in ((0, acc_k), (1, acc_v)):
            left_grads[half] = acc[:rim, :].astype(jnp.bfloat16)
            right_grads[half] = acc[rim + rows :, :].astype(jnp.bfloat16)
            own_grads[half] = acc[rim : rim + rows, :]
        count, both, _ = terms.shape
        cut = both // 2
        terms[:, :cut, :] = acc_q[...].astype(jnp.bfloat16).reshape(count, cut, BLK)
        terms[:, cut:, :] = acc_o[...].astype(jnp.bfloat16).reshape(count, cut, BLK)


def combine_kernel(own, from_left, from_right, out):
    rows, rim = own.shape[1], from_left.shape[1]
    for half in range(2):
        for first in range(0, rows, CHUNK):
            part = own[half, first : first + CHUNK, :]
            if first < rim:
                part = part + from_left[half, first : first + CHUNK, :].astype(jnp.float32)
            if first >= rows - rim:
                start = first - (rows - rim)
                part = part + from_right[half, start : start + CHUNK, :].astype(jnp.float32)
            out[half, first : first + CHUNK, :] = part.astype(jnp.bfloat16)


def params(limit=VMEM_LIMIT):
    return pltpu.CompilerParams(dimension_semantics=("arbitrary",), vmem_limit_bytes=limit)


ANYWHERE = pl.BlockSpec(memory_space=pl.ANY)
ROW_BLOCK = pl.BlockSpec((BLK, BLK), lambda i: (i, 0))
INVERSE = pl.BlockSpec((1, 8, 2 * BLK), lambda i: (i, 0, 0))


def flip_keys_values(left, own, right):
    rim, rows = left.shape[1], own.shape[1]
    ext = 2 * rim + rows
    half = lambda size: pl.BlockSpec((1, size, BLK), lambda i: (i, 0, 0))
    return pl.pallas_call(
        transpose_kernel,
        grid=(2,),
        in_specs=[half(rim), half(rows), half(rim)],
        out_specs=pl.BlockSpec((1, BLK, ext), lambda i: (i, 0, 0)),
        out_shape=jax.ShapeDtypeStruct((2, BLK, ext), jnp.bfloat16),
        compiler_params=params(),
        cost_estimate=pl.CostEstimate(flops=0, bytes_accessed=8_000_000, transcendentals=0),
        name="flip_keys_values",
    )(left, own, right)


def attention_forward(bias, x, weight, left, own, right, flipped, step_rows, window):
    blocks = x.shape[0] // BLK
    width = x.shape[1]
    ext = flipped.shape[2]
    chunks = window // CHUNK
    return pl.pallas_call(
        functools.partial(forward_kernel, step_rows, window, DH ** -0.5),
        grid=(blocks,),
        in_specs=[
            pl.BlockSpec(memory_space=pltpu.SMEM),
            pl.BlockSpec((BLK, width), lambda i: (i, 0)),
            pl.BlockSpec(weight.shape, lambda i: (0, 0)),
        ] + [ANYWHERE] * 4,
        out_specs=[
            pl.BlockSpec((1, window, 2 * BLK), lambda i: (i, 0, 0)),
            ROW_BLOCK,
            pl.BlockSpec((1, chunks, 2 * BLK), lambda i: (i, 0, 0)),
            ROW_BLOCK,
        ],
        out_shape=[
            jax.ShapeDtypeStruct((blocks, window, 2 * BLK), jnp.bfloat16),
            jax.ShapeDtypeStruct((blocks * BLK, BLK), jnp.bfloat16),
            jax.ShapeDtypeStruct((blocks, chunks, 2 * BLK), jnp.float32),
            jax.ShapeDtypeStruct((blocks * BLK, BLK), jnp.bfloat16),
        ],
        scratch_shapes=[
            pltpu.VMEM((ext, BLK), jnp.bfloat16),
            pltpu.VMEM((BLK, ext), jnp.bfloat16),
            pltpu.VMEM((chunks, BLK, 2 * BLK), jnp.float32),
            pltpu.SemaphoreType.DMA((3,)),
            pltpu.SemaphoreType.DMA,
        ],
        compiler_params=params(),
        cost_estimate=pl.CostEstimate(
            flops=blocks * 16 * window * BLK * BLK * 2, bytes_accessed=14_000_000,
            transcendentals=blocks * window * 2 * BLK,
        ),
        name="attention_forward",
    )(bias, x, weight, left, own, right, flipped)


def attention_backward(x, g, weight, queries, attn, factor, probs, left, own, right, flipped, step_rows, parts):
    blocks, window, _ = probs.shape
    width = x.shape[1]
    rim, rows = left.shape[1], own.shape[1]
    ext = flipped.shape[2]
    whole = lambda *shape: pl.BlockSpec(shape, lambda i: (0,) * len(shape))
    row_wide = pl.BlockSpec((BLK, width), lambda i: (i, 0))
    both = 2 * width // parts
    return pl.pallas_call(
        functools.partial(backward_kernel, step_rows, window, DH ** -0.5),
        grid=(blocks,),
        in_specs=[
            row_wide, row_wide, whole(*weight.shape), ROW_BLOCK, ROW_BLOCK,
            pl.BlockSpec((1,) + factor.shape[1:], lambda i: (i, 0, 0)),
            pl.BlockSpec((1, window, 2 * BLK), lambda i: (i, 0, 0)),
        ] + [ANYWHERE] * 4,
        out_specs=[
            ROW_BLOCK, whole(2, rows, BLK), whole(2, rim, BLK), whole(2, rim, BLK), whole(parts, both, BLK),
        ],
        out_shape=[
            jax.ShapeDtypeStruct(attn.shape, jnp.bfloat16),
            jax.ShapeDtypeStruct((2, rows, BLK), jnp.float32),
            jax.ShapeDtypeStruct((2, rim, BLK), jnp.bfloat16),
            jax.ShapeDtypeStruct((2, rim, BLK), jnp.bfloat16),
            jax.ShapeDtypeStruct((parts, both, BLK), jnp.bfloat16),
        ],
        scratch_shapes=[
            pltpu.VMEM((ext, BLK), jnp.bfloat16),
            pltpu.VMEM((BLK, ext), jnp.bfloat16),
            pltpu.VMEM((ext, BLK), jnp.float32),
            pltpu.VMEM((ext, BLK), jnp.float32),
            pltpu.VMEM((width, BLK), jnp.float32),
            pltpu.VMEM((width, BLK), jnp.float32),
            pltpu.SemaphoreType.DMA((3,)),
            pltpu.SemaphoreType.DMA,
        ],
        compiler_params=params(),
        cost_estimate=pl.CostEstimate(
            flops=blocks * 20 * window * BLK * BLK * 2, bytes_accessed=20_000_000, transcendentals=0
        ),
        name="attention_backward",
    )(x, g, weight, queries, attn, factor, probs, left, own, right, flipped)


def combine_grads(own, from_left, from_right):
    return pl.pallas_call(
        combine_kernel,
        out_shape=jax.ShapeDtypeStruct(own.shape, jnp.bfloat16),
        compiler_params=pltpu.CompilerParams(vmem_limit_bytes=VMEM_LIMIT),
        cost_estimate=pl.CostEstimate(flops=1_000_000, bytes_accessed=8_000_000, transcendentals=0),
        name="combine_grads",
    )(own, from_left, from_right)


def shifted(count, by):
    return [(i, (i + by) % count) for i in range(count)]


def ring_gather(shard, axis, ready, at_step):
    count = lax.axis_size(axis)
    here = lax.axis_index(axis)
    rows = shard.shape[0]
    pieces = [(shard, 0)]
    forward = backward = shard
    for step in range(1, count // 2 + 1):
        if step == at_step:
            forward, backward, ready = lax.optimization_barrier((forward, backward, ready))
        forward = lax.ppermute(forward, axis, shifted(count, 1))
        pieces.append((forward, -step))
        if step < count - step:
            backward = lax.ppermute(backward, axis, shifted(count, -1))
            pieces.append((backward, step))
    out = jnp.zeros((count * rows,) + shard.shape[1:], shard.dtype)
    for piece, by in pieces:
        out = lax.dynamic_update_slice_in_dim(out, piece, lax.rem(here + by + count, count) * rows, 0)
    return out, ready


def band_bias(band_lists, base_block, query_blocks, half_step, reach_blocks):
    local = jnp.arange(query_blocks, dtype=jnp.int32)
    window_first = base_block + (2 * local + 1) * half_step - reach_blocks
    wanted = window_first[:, None] + jnp.arange(2 * reach_blocks, dtype=jnp.int32)[None, :]
    allowed = jnp.any(band_lists[:, :, None] == wanted[:, None, :], axis=1)
    return jnp.where(allowed, 0.0, MASKED).astype(jnp.float32)


def added(arrived):
    return jnp.sum(arrived.astype(jnp.float32), axis=0, keepdims=True).astype(jnp.bfloat16)


def exchange(parts, axis):
    return lax.all_to_all(parts, axis, 0, 0, tiled=True)


def on_device(slow_x, q_weight, o_weight, fast_kv, mask_lists, cotangent):
    own_rows, width = slow_x.shape
    tp = lax.axis_size("tp")
    ctx = lax.axis_size("ctx")
    total_rows = own_rows * tp
    query_blocks = total_rows // BLK
    fast_rows = fast_kv.shape[1]
    fast_blocks = fast_rows // BLK
    half_step = fast_blocks // (2 * query_blocks)
    reach_blocks = mask_lists.shape[1] // 2
    rim = (reach_blocks - half_step) * BLK
    window = 2 * reach_blocks * BLK
    step_rows = 2 * half_step * BLK
    scale = DH ** -0.5

    up = [(i, i + 1) for i in range(ctx - 1)]
    down = [(i + 1, i) for i in range(ctx - 1)]
    left = lax.ppermute(fast_kv[:, fast_rows - rim :], "ctx", up)
    right = lax.ppermute(fast_kv[:, :rim], "ctx", down)

    rows_g = lax.all_gather(cotangent, "tp", axis=0, tiled=True)
    ctx_index = lax.axis_index("ctx")
    even = ctx_index % 2 == 0
    band_lists = lax.dynamic_slice_in_dim(mask_lists, ctx_index * query_blocks, query_blocks, 0)
    bias = band_bias(band_lists, ctx_index * fast_blocks, query_blocks, half_step, reach_blocks)
    shard = jnp.where(even, o_weight, q_weight.T)
    flipped = flip_keys_values(left, fast_kv, right)
    rows_x, (flipped, bias, shard) = ring_gather(slow_x, "tp", (flipped, bias, shard), 3)

    probs, attn, factor, queries = attention_forward(
        bias, rows_x, q_weight, left, fast_kv, right, flipped, step_rows, window
    )
    shard, rows_g, attn = lax.optimization_barrier((shard, rows_g, attn))
    mine = lax.all_gather(shard, "tp", axis=0, tiled=True)
    grad_pre, own_grads, left_grads, right_grads, terms = attention_backward(
        rows_x, rows_g, o_weight, queries, attn, factor, probs, left, fast_kv, right, flipped, step_rows, ctx
    )
    own_terms = added(exchange(terms, "ctx"))
    mine, own_terms = lax.optimization_barrier((mine, own_terms))
    other = lax.ppermute(mine, "ctx", [(i, i ^ 1) for i in range(ctx)])
    from_right = lax.ppermute(left_grads, "ctx", down)
    from_left = lax.ppermute(right_grads, "ctx", up)
    mixed = jnp.concatenate([attn, grad_pre], axis=1).reshape(tp, own_rows, 2 * BLK)
    mixed = exchange(mixed, "tp")
    summed = exchange(jnp.broadcast_to(own_terms, terms.shape), "ctx")
    grad_kv = combine_grads(own_grads, from_left, from_right)

    first = jnp.where(even, mixed[:, :, :BLK], mixed[:, :, BLK:])
    second = jnp.where(even, mixed[:, :, BLK:], mixed[:, :, :BLK])
    project = lambda rows, full: jnp.einsum(
        "trk,tkn->rn", rows, full.reshape(tp, BLK, width), preferred_element_type=jnp.float32
    ).astype(jnp.bfloat16)
    first = project(first, mine)
    second = project(second, other)
    attended = jnp.where(even, first, second)
    grad_slow = jnp.where(even, second, first)

    cut = terms.shape[1] // 2
    grad_q_weight = summed[:, :cut].astype(jnp.float32).reshape(q_weight.shape)
    grad_o_weight = summed[:, cut:].astype(jnp.float32).reshape(q_weight.shape).T
    return (attended, grad_slow, grad_q_weight, grad_o_weight, grad_kv)


def solution(mesh):
    in_specs = (
        P(("ctx", "tp"), None),
        P(None, "tp"),
        P("tp", None),
        P(None, "ctx", "tp"),
        P(),
        P(("ctx", "tp"), None),
    )
    out_specs = (
        P(("ctx", "tp"), None),
        P(("ctx", "tp"), None),
        P(None, "tp"),
        P("tp", None),
        P(None, "ctx", "tp"),
    )
    return jax.shard_map(on_device, mesh=mesh, in_specs=in_specs, out_specs=out_specs, check_vma=False)
```

```python
import functools

import jax
import jax.numpy as jnp
from jax import lax
from jax.experimental import pallas as pl
from jax.experimental.pallas import tpu as pltpu
from jax.sharding import PartitionSpec as P

BLK = 128
DH = 64
CHUNK = 512
MASKED = -1e30
VMEM_LIMIT = 58 * 1024 * 1024


def contract(a, b, dims):
    return lax.dot_general(a, b, (dims, ((), ())), preferred_element_type=jnp.float32)


def row_split(block):
    lane = lax.broadcasted_iota(jnp.int32, block.shape, 1)
    zero = jnp.zeros_like(block)
    return jnp.concatenate([jnp.where(lane < DH, block, zero), jnp.where(lane >= DH, block, zero)], axis=0)


def column_split(block):
    row = lax.broadcasted_iota(jnp.int32, block.shape, 0)
    zero = jnp.zeros_like(block)
    return jnp.concatenate([jnp.where(row < DH, block, zero), jnp.where(row >= DH, block, zero)], axis=1)


def column_join(wide):
    row = lax.broadcasted_iota(jnp.int32, (wide.shape[0], BLK), 0)
    return jnp.where(row < DH, wide[:, :BLK], wide[:, BLK:])


def spread_kernel(fill, *refs):
    pieces = refs[: len(fill)]
    natural, flipped = refs[-(len(fill) + 3) : -(len(fill) + 1)]
    turned, sems = refs[-(len(fill) + 1) : -1], refs[-1]
    copies = []
    for number, (piece, first) in enumerate(zip(pieces, fill)):
        rows = piece.shape[1]
        copies.append(pltpu.make_async_copy(piece, natural.at[:, pl.ds(first, rows)], sems.at[number, 0]))
        copies[-1].start()
    for number, (piece, first) in enumerate(zip(pieces, fill)):
        rows = piece.shape[1]
        for half in range(2):
            for row in range(0, rows, CHUNK):
                turned[number][half, :, row : row + CHUNK] = piece[half, row : row + CHUNK, :].T
            copies.append(
                pltpu.make_async_copy(
                    turned[number].at[half], flipped.at[half, :, pl.ds(first, rows)], sems.at[number, 1 + half]
                )
            )
            copies[-1].start()
    for copy in copies:
        copy.wait()


def pair_kernel(step_rows, window, scale, turn, moved, place, bias, lo_even, lo_odd, hi_even, hi_odd,
                q_weight, o_weight, natural, flipped, *rest):
    pieces, rest = rest[: len(moved)], rest[len(moved) :]
    (grads, mixed, rows_out, weights, keys, values, keys_t, values_t, probs, parts, grad_out, mixed_out, x_rows, g_rows,
     through, sems_in, sems_out, sems_row, sems_piece) = rest if turn == 0 else rest[4:]
    chunks, per = window // CHUNK, CHUNK // BLK
    pair = place[turn, 0]
    even = place[turn, 1] == 0
    start = pl.multiple_of(pair * step_rows, step_rows)
    span = pl.ds(start, window)
    copies = [
        pltpu.make_async_copy(natural.at[0, span], keys, sems_in.at[0]),
        pltpu.make_async_copy(flipped.at[1, :, span], values_t, sems_in.at[1]),
        pltpu.make_async_copy(natural.at[1, span], values, sems_in.at[2]),
        pltpu.make_async_copy(flipped.at[0, :, span], keys_t, sems_in.at[3]),
    ]
    for copy in copies:
        copy.start()
    half_rows = BLK // 2

    def fetch(lo, hi):
        return [
            pltpu.make_async_copy(
                source.at[pl.ds(part * half_rows, half_rows)], dest.at[pl.ds(side * half_rows, half_rows)],
                sems_row.at[2 + 2 * part + side],
            )
            for part, dest in enumerate((x_rows, g_rows))
            for side, source in enumerate((lo, hi))
        ]

    @pl.when(even)
    def _():
        for copy in fetch(lo_even, hi_even):
            copy.start()

    @pl.when(jnp.logical_not(even))
    def _():
        for copy in fetch(lo_odd, hi_odd):
            copy.start()

    arriving = [
        pltpu.make_async_copy(piece.at[pl.ds(first, BLK)], through.at[number], sems_piece.at[0, number])
        for number, (piece, (_, first)) in enumerate(zip(pieces, moved))
    ]
    for copy in arriving:
        copy.start()
    kept = []
    for copy in fetch(lo_even, hi_even):
        copy.wait()
    out_rows = pl.ds(pl.multiple_of(pair * BLK, BLK), BLK)
    for part, source in enumerate((x_rows, g_rows)):
        copy = pltpu.make_async_copy(source, rows_out.at[part, out_rows], sems_row.at[part])
        copy.start()
        kept.append(copy)

    q = (contract(x_rows[...], q_weight[...], ((1,), (0,))) * scale).astype(jnp.bfloat16)
    grad = contract(g_rows[...], o_weight[...], ((1,), (1,))).astype(jnp.bfloat16).astype(jnp.float32)
    q_t = column_split(q.T)
    query_rows = row_split(q)
    grad_t = grad.T
    wide, tall = column_split(grad_t), row_split(grad)

    at = lambda c: slice(c * CHUNK, (c + 1) * CHUNK)
    scores = lambda c: contract(keys[at(c), :], q_t, ((1,), (0,)))
    fold = lambda t, op: op(op(t.reshape(CHUNK // 8, 8, 2 * BLK), axis=0), axis=0, keepdims=True)

    def weigh(c, half):
        parts[c] = contract(values_t[:, at(c)], half, ((1,), (0,)))

    copies[0].wait()
    tops, sums = [], []
    ahead, held = scores(0), None
    copies[1].wait()
    for c in range(chunks):
        s = ahead
        if c + 1 < chunks:
            ahead = scores(c + 1)
        s = jnp.concatenate([s[j * BLK : (j + 1) * BLK] + bias[pair, c * per + j] for j in range(per)], axis=0)
        top = fold(s, jnp.max)
        e = jnp.exp(s - top)
        tops.append(top)
        sums.append(fold(e, jnp.sum))
        half = e.astype(jnp.bfloat16)
        probs[at(c), :] = half
        if held is not None:
            weigh(c - 1, held)
        held = half
    weigh(chunks - 1, held)
    tops = jnp.concatenate(tops, axis=0)
    sums = jnp.concatenate(sums, axis=0)
    f = jnp.exp(tops - jnp.max(tops, axis=0, keepdims=True))
    f = f * (1.0 / jnp.sum(f * sums, axis=0, keepdims=True))
    out = parts[0] * f[:1]
    for c in range(1, chunks):
        out = out + parts[c] * f[c : c + 1]
    attn = column_join(out).T.astype(jnp.bfloat16)
    mixed_out[:, :BLK] = attn

    product = grad_t * attn.astype(jnp.float32).T
    delta = jnp.concatenate(
        [jnp.sum(product[:DH], axis=0, keepdims=True), jnp.sum(product[DH:], axis=0, keepdims=True)], axis=1
    )
    f_t = f.T
    homes = weights.shape[0]
    for number, (by, _) in enumerate(moved):
        arriving[number].wait()
        home = lax.rem(place[turn, 2] + (by + homes), homes)
        copy = pltpu.make_async_copy(through.at[number], weights.at[home], sems_piece.at[1, number])
        copy.start()
        kept.append(copy)
    copies[2].wait()
    copies[3].wait()
    lift = lambda c: contract(values[at(c), :], (wide * f[c : c + 1]).astype(jnp.bfloat16), ((1,), (0,)))
    total = jnp.zeros((BLK, 2 * BLK), jnp.float32)
    ahead = lift(0)
    sent = []
    for c in range(chunks):
        dp = ahead
        if c + 1 < chunks:
            ahead = lift(c + 1)
        e = probs[at(c), :]
        ds = (e.astype(jnp.float32) * (dp - delta * f[c : c + 1])).astype(jnp.bfloat16)
        total = total + contract(keys_t[:, at(c)], ds, ((1,), (0,)))
        grad_out[0, at(c), :] = contract(ds, query_rows, ((1,), (0,))).astype(jnp.bfloat16)
        grad_out[1, at(c), :] = contract(
            e, (tall * f_t[:, c : c + 1]).astype(jnp.bfloat16), ((1,), (0,))
        ).astype(jnp.bfloat16)
        piece = pl.ds(c * CHUNK, CHUNK)
        copy = pltpu.make_async_copy(grad_out.at[:, piece], grads.at[pair, :, piece], sems_out.at[c])
        copy.start()
        sent.append(copy)
    mixed_out[:, BLK:] = (column_join(total) * scale).T.astype(jnp.bfloat16)
    copy = pltpu.make_async_copy(mixed_out, mixed.at[out_rows], sems_row.at[6])
    copy.start()
    for copy in sent + kept + [copy]:
        copy.wait()


def terms_kernel(rows, mixed, out):
    attn = mixed[:, :BLK]
    pre = mixed[:, BLK:]
    by_query = contract(pre, rows[0], ((0,), (0,))).T.astype(jnp.bfloat16)
    by_output = contract(attn, rows[1], ((0,), (0,))).astype(jnp.bfloat16)
    count, both, _ = out.shape
    cut = both // 2
    groups = BLK // cut
    for i in range(count):
        out[i, :cut, :] = by_query[i * cut : (i + 1) * cut, :]
        row, column = (i % groups) * cut, (i // groups) * BLK
        out[i, cut:, :] = by_output[row : row + cut, column : column + BLK]


def rim_kernel(step_rows, grads, left_out, right_out, far_l, near_l, far_r, near_r, sems):
    blocks, _, window, _ = grads.shape
    rim = left_out.shape[1]
    overlap = rim - step_rows
    copies = [
        pltpu.make_async_copy(grads.at[0, :, pl.ds(0, rim)], far_l, sems.at[0]),
        pltpu.make_async_copy(grads.at[1, :, pl.ds(0, overlap)], near_l, sems.at[1]),
        pltpu.make_async_copy(grads.at[blocks - 1, :, pl.ds(window - rim, rim)], far_r, sems.at[2]),
        pltpu.make_async_copy(grads.at[blocks - 2, :, pl.ds(window - overlap, overlap)], near_r, sems.at[3]),
    ]
    for copy in copies:
        copy.start()
    for copy in copies:
        copy.wait()
    add = lambda a, b: (a.astype(jnp.float32) + b.astype(jnp.float32)).astype(jnp.bfloat16)
    left_out[:, :step_rows, :] = far_l[:, :step_rows, :]
    left_out[:, step_rows:, :] = add(far_l[:, step_rows:, :], near_l[...])
    right_out[:, :overlap, :] = add(far_r[:, :overlap, :], near_r[...])
    right_out[:, overlap:, :] = far_r[:, overlap:, :]


def combine_kernel(step_rows, grads, from_left, from_right, out, held, result, sems, sems_out):
    blocks, _, window, _ = grads.shape
    rows, rim = out.shape[1], from_left.shape[1]
    plan = []
    slot = 0
    for first in range(0, rows, CHUNK):
        sources = []
        for block in range(blocks):
            local = first + rim - block * step_rows
            if 0 <= local < window:
                sources.append((grads.at[block, :, pl.ds(local, CHUNK)], slot))
                slot += 1
        if first < rim:
            sources.append((from_left.at[:, pl.ds(first, CHUNK)], slot))
            slot += 1
        if first >= rows - rim:
            sources.append((from_right.at[:, pl.ds(first - (rows - rim), CHUNK)], slot))
            slot += 1
        copies = [pltpu.make_async_copy(source, held.at[n], sems.at[n]) for source, n in sources]
        for copy in copies:
            copy.start()
        plan.append((first, sources, copies))
    sent = []
    for number, (first, sources, copies) in enumerate(plan):
        for copy in copies:
            copy.wait()
        part = held[sources[0][1]].astype(jnp.float32)
        for _, n in sources[1:]:
            part = part + held[n].astype(jnp.float32)
        result[:, first : first + CHUNK, :] = part.astype(jnp.bfloat16)
        piece = pl.ds(first, CHUNK)
        copy = pltpu.make_async_copy(result.at[:, piece], out.at[:, piece], sems_out.at[number])
        copy.start()
        sent.append(copy)
    for copy in sent:
        copy.wait()


ANYWHERE = pl.BlockSpec(memory_space=pl.ANY)
IN_VMEM = pl.BlockSpec(memory_space=pltpu.VMEM)
IN_SMEM = pl.BlockSpec(memory_space=pltpu.SMEM)


def params():
    return pltpu.CompilerParams(vmem_limit_bytes=VMEM_LIMIT)


def cost(flops, moved, exps=0):
    return pl.CostEstimate(flops=flops, bytes_accessed=moved, transcendentals=exps)


def pack_kernel(flag, x, g, o_weight, q_weight, kv, out, tail, head, sems):
    rows = x.shape[0]
    span, rim = kv.shape[1], tail.shape[1]
    copies = [
        pltpu.make_async_copy(kv.at[:, pl.ds(span - rim, rim)], tail, sems.at[0]),
        pltpu.make_async_copy(kv.at[:, pl.ds(0, rim)], head, sems.at[1]),
    ]
    for copy in copies:
        copy.start()
    out[:rows, :] = x[...]
    out[rows : 2 * rows, :] = g[...]

    @pl.when(flag[0] == 0)
    def _():
        out[2 * rows :, :] = o_weight[...]

    @pl.when(flag[0] != 0)
    def _():
        out[2 * rows :, :] = q_weight[...].T

    for copy in copies:
        copy.wait()


def pack(flag, x, g, o_weight, q_weight, kv, rim):
    edge = jax.ShapeDtypeStruct((2, rim, BLK), kv.dtype)
    return pl.pallas_call(
        pack_kernel,
        in_specs=[IN_SMEM] + [IN_VMEM] * 4 + [ANYWHERE],
        out_specs=[IN_VMEM] * 3,
        out_shape=[jax.ShapeDtypeStruct((2 * x.shape[0] + o_weight.shape[0], x.shape[1]), x.dtype), edge, edge],
        scratch_shapes=[pltpu.SemaphoreType.DMA((2,))],
        cost_estimate=cost(0, 4_000_000),
        name="pack",
    )(flag, x, g, o_weight, q_weight, kv)


def spread_rows(pieces, fill, ext, carried, name):
    extra = () if carried is None else tuple(carried)
    return pl.pallas_call(
        functools.partial(spread_kernel, fill),
        in_specs=[IN_VMEM] * len(pieces) + [ANYWHERE] * len(extra),
        out_specs=[ANYWHERE] * 2,
        out_shape=[
            jax.ShapeDtypeStruct((2, ext, BLK), jnp.bfloat16),
            jax.ShapeDtypeStruct((2, BLK, ext), jnp.bfloat16),
        ],
        input_output_aliases={len(pieces) + i: i for i in range(len(extra))},
        scratch_shapes=[pltpu.VMEM((2, BLK, piece.shape[1]), jnp.bfloat16) for piece in pieces]
        + [pltpu.SemaphoreType.DMA((len(pieces), 3))],
        compiler_params=params(),
        cost_estimate=cost(0, 8_000_000),
        name=name,
    )(*pieces, *extra)


def attention_pair(turn, place, bias, shards, moved, q_weight, o_weight, natural, flipped, carried, blocks, homes,
                   step_rows, window):
    width = q_weight.shape[0]
    chunks = window // CHUNK
    shapes = [
        jax.ShapeDtypeStruct((blocks, 2, window, BLK), jnp.bfloat16),
        jax.ShapeDtypeStruct((blocks * BLK, 2 * BLK), jnp.bfloat16),
        jax.ShapeDtypeStruct((2, blocks * BLK, width), jnp.bfloat16),
        jax.ShapeDtypeStruct((homes, BLK, width), jnp.bfloat16),
    ]
    extra = () if carried is None else tuple(carried)
    pieces = [piece for piece, _, _ in moved]
    first_extra = 10 + len(pieces)
    bf = lambda *shape: pltpu.VMEM(shape, jnp.bfloat16)
    return pl.pallas_call(
        functools.partial(pair_kernel, step_rows, window, DH ** -0.5, turn, [m[1:] for m in moved]),
        in_specs=[IN_SMEM, IN_SMEM] + [ANYWHERE] * 4 + [IN_VMEM] * 2 + [ANYWHERE] * (2 + len(pieces) + len(extra)),
        out_specs=[ANYWHERE] * 4,
        out_shape=shapes,
        input_output_aliases={first_extra + i: i for i in range(len(extra))},
        scratch_shapes=[
            bf(window, BLK), bf(window, BLK), bf(BLK, window), bf(BLK, window),
            bf(window, 2 * BLK), pltpu.VMEM((chunks, BLK, 2 * BLK), jnp.float32),
            bf(2, window, BLK), bf(BLK, 2 * BLK), bf(BLK, width), bf(BLK, width), bf(len(pieces), BLK, width),
            pltpu.SemaphoreType.DMA((4,)), pltpu.SemaphoreType.DMA((chunks,)), pltpu.SemaphoreType.DMA((7,)),
            pltpu.SemaphoreType.DMA((2, len(pieces))),
        ],
        compiler_params=params(),
        cost_estimate=cost(4_000_000_000, 10_000_000, window * 2 * BLK),
        name="attention_pair",
    )(place, bias, *shards, q_weight, o_weight, natural, flipped, *pieces, *extra)


def weight_terms(rows, mixed, parts):
    width = rows.shape[2]
    return pl.pallas_call(
        terms_kernel,
        in_specs=[IN_VMEM] * 2,
        out_specs=IN_VMEM,
        out_shape=jax.ShapeDtypeStruct((parts, 2 * width // parts, BLK), jnp.bfloat16),
        compiler_params=params(),
        cost_estimate=cost(1_000_000_000, 4_000_000),
        name="weight_terms",
    )(rows, mixed)


def rim_grads(grads, rim, step_rows):
    bf = lambda rows: pltpu.VMEM((2, rows, BLK), jnp.bfloat16)
    edge = jax.ShapeDtypeStruct((2, rim, BLK), jnp.bfloat16)
    return pl.pallas_call(
        functools.partial(rim_kernel, step_rows),
        in_specs=[ANYWHERE],
        out_specs=[IN_VMEM] * 2,
        out_shape=[edge, edge],
        scratch_shapes=[bf(rim), bf(rim - step_rows), bf(rim), bf(rim - step_rows), pltpu.SemaphoreType.DMA((4,))],
        compiler_params=params(),
        cost_estimate=cost(1_000_000, 5_000_000),
        name="rim_grads",
    )(grads)


def combine_grads(grads, from_left, from_right, rows, step_rows):
    blocks, _, window, _ = grads.shape
    rim = from_left.shape[1]
    inside = sum(
        0 <= first + rim - block * step_rows < window for first in range(0, rows, CHUNK) for block in range(blocks)
    )
    slots = inside + 2 * (rim // CHUNK)
    return pl.pallas_call(
        functools.partial(combine_kernel, step_rows),
        in_specs=[ANYWHERE] * 3,
        out_specs=ANYWHERE,
        out_shape=jax.ShapeDtypeStruct((2, rows, BLK), jnp.bfloat16),
        scratch_shapes=[
            pltpu.VMEM((slots, 2, CHUNK, BLK), jnp.bfloat16),
            pltpu.VMEM((2, rows, BLK), jnp.bfloat16),
            pltpu.SemaphoreType.DMA((slots,)),
            pltpu.SemaphoreType.DMA((rows // CHUNK,)),
        ],
        compiler_params=params(),
        cost_estimate=cost(5_000_000, 10_000_000),
        name="combine_grads",
    )(grads, from_left, from_right)


def unpack_kernel(summed, q_out, o_out):
    count, both, _ = summed.shape
    cut = both // 2
    groups = BLK // cut
    for i in range(count):
        q_out[i * cut : (i + 1) * cut, :] = summed[i, :cut, :].astype(jnp.float32)
        row, column = (i % groups) * cut, (i // groups) * BLK
        o_out[row : row + cut, column : column + BLK] = summed[i, cut:, :].astype(jnp.float32)


def unpack_terms(summed, q_shape, o_shape):
    return pl.pallas_call(
        unpack_kernel,
        out_shape=[jax.ShapeDtypeStruct(q_shape, jnp.float32), jax.ShapeDtypeStruct(o_shape, jnp.float32)],
        cost_estimate=cost(0, 1_500_000),
        name="unpack_terms",
    )(summed)


def shifted(count, by):
    return [(i, (i + by) % count) for i in range(count)]


def band_bias(band_lists, base_block, query_blocks, half_step, reach_blocks):
    local = jnp.arange(query_blocks, dtype=jnp.int32)
    window_first = base_block + (2 * local + 1) * half_step - reach_blocks
    wanted = window_first[:, None] + jnp.arange(2 * reach_blocks, dtype=jnp.int32)[None, :]
    allowed = jnp.any(band_lists[:, :, None] == wanted[:, None, :], axis=1)
    return jnp.where(allowed, 0.0, MASKED).astype(jnp.float32)


def added(arrived):
    return jnp.sum(arrived.astype(jnp.float32), axis=0, keepdims=True).astype(jnp.bfloat16)


def exchange(parts, axis):
    return lax.all_to_all(parts, axis, 0, 0, tiled=True)


def on_device(slow_x, q_weight, o_weight, fast_kv, mask_lists, cotangent):
    own_rows, width = slow_x.shape
    tp = lax.axis_size("tp")
    ctx = lax.axis_size("ctx")
    total_rows = own_rows * tp
    query_blocks = total_rows // BLK
    fast_rows = fast_kv.shape[1]
    fast_blocks = fast_rows // BLK
    half_step = fast_blocks // (2 * query_blocks)
    reach_blocks = mask_lists.shape[1] // 2
    rim = (reach_blocks - half_step) * BLK
    window = 2 * reach_blocks * BLK
    step_rows = 2 * half_step * BLK

    ctx_index = lax.axis_index("ctx")
    flag = (ctx_index % 2).reshape(1).astype(jnp.int32)
    own, tail, head = pack(flag, slow_x, cotangent, o_weight, q_weight, fast_kv, rim)
    up = [(i, i + 1) for i in range(ctx - 1)]
    down = [(i + 1, i) for i in range(ctx - 1)]
    left = lax.ppermute(tail, "ctx", up)
    right = lax.ppermute(head, "ctx", down)

    even = ctx_index % 2 == 0
    band_lists = lax.dynamic_slice_in_dim(mask_lists, ctx_index * query_blocks, query_blocks, 0)
    bias = band_bias(band_lists, ctx_index * fast_blocks, query_blocks, half_step, reach_blocks)
    ext = 2 * rim + fast_rows
    spread_own = spread_rows([fast_kv], [rim], ext, None, "spread_own")
    natural, flipped = spread_rows([left, right], [0, rim + fast_rows], ext, spread_own, "spread_rims")

    tp_index = lax.axis_index("tp")
    parity = tp_index % 2
    turn = 1 - 2 * parity
    middle = tp_index // 2
    moves = jnp.array([0, 0, 0, 2], jnp.int32) + jnp.array([0, -1, 1, 0], jnp.int32) * turn
    pairs = (middle + moves + query_blocks) % query_blocks
    spread = lambda value: jnp.broadcast_to(value, pairs.shape)
    place = jnp.stack([pairs, spread(parity), spread(tp_index)], axis=1).astype(jnp.int32)
    ahead, behind = shifted(tp, 1), shifted(tp, -1)
    shared = 2 * own_rows
    f, b = [own], [own]

    def pass_on(gate):
        back, front = f[-1], b[-1]
        if gate is not None:
            back, front, gate = lax.optimization_barrier((back, front, gate))
        if 2 * len(f) < tp:
            f.append(lax.ppermute(back, "tp", ahead))
            b.append(lax.ppermute(front, "tp", behind))
        else:
            f.append(lax.ppermute(back[:shared], "tp", ahead))
            b.append(lax.ppermute(front[shared:], "tp", behind))
        return gate

    picks = [
        lambda: ((own, f[1], b[1], own), [(own, 0, shared), (f[1], -1, shared), (b[1], 1, shared)]),
        lambda: ((f[2], b[1], f[1], b[2]), [(f[2], -2, shared), (b[2], 2, shared)]),
        lambda: ((b[2], f[3], b[3], f[2]), [(f[3], -3, shared), (b[3], 3, shared)]),
        lambda: ((f[4], b[3], f[3], f[4]), [(b[4], 4, 0)]),
    ]
    pass_on(None)
    pass_on(None)
    carried = None
    for number, pick in enumerate(picks):
        shards, moved = pick()
        carried = attention_pair(
            number, place, bias, shards, moved, q_weight, o_weight, natural, flipped, carried, query_blocks, tp,
            step_rows, window,
        )
        if len(f) <= tp // 2:
            carried = (carried[0], pass_on(carried[1])) + tuple(carried[2:])
    grads, rows_mixed, rows_all, mine = carried

    mixed = exchange(rows_mixed.reshape(tp, own_rows, 2 * BLK), "tp")
    terms = weight_terms(rows_all, rows_mixed, ctx)
    left_grads, right_grads = rim_grads(grads, rim, step_rows)
    terms, left_grads, right_grads, mixed = lax.optimization_barrier((terms, left_grads, right_grads, mixed))
    own_terms = added(exchange(terms, "ctx"))
    from_right = lax.ppermute(left_grads, "ctx", down)
    from_left = lax.ppermute(right_grads, "ctx", up)
    other = lax.ppermute(mine, "ctx", [(i, i ^ 1) for i in range(ctx)])
    summed = exchange(jnp.broadcast_to(own_terms, terms.shape), "ctx")
    grad_kv = combine_grads(grads, from_left, from_right, fast_rows, step_rows)

    first = jnp.where(even, mixed[:, :, :BLK], mixed[:, :, BLK:])
    second = jnp.where(even, mixed[:, :, BLK:], mixed[:, :, :BLK])
    project = lambda rows, full: jnp.einsum(
        "trk,tkn->rn", rows, full.reshape(tp, BLK, width), preferred_element_type=jnp.float32
    ).astype(jnp.bfloat16)
    first = project(first, mine)
    second = project(second, other)
    attended = jnp.where(even, first, second)
    grad_slow = jnp.where(even, second, first)

    summed, attended, grad_slow, grad_kv = lax.optimization_barrier((summed, attended, grad_slow, grad_kv))
    grad_q_weight, grad_o_weight = unpack_terms(summed, q_weight.shape, o_weight.shape)
    return (attended, grad_slow, grad_q_weight, grad_o_weight, grad_kv)


def solution(mesh):
    in_specs = (
        P(("ctx", "tp"), None),
        P(None, "tp"),
        P("tp", None),
        P(None, "ctx", "tp"),
        P(),
        P(("ctx", "tp"), None),
    )
    out_specs = (
        P(("ctx", "tp"), None),
        P(("ctx", "tp"), None),
        P(None, "tp"),
        P("tp", None),
        P(None, "ctx", "tp"),
    )
    return jax.shard_map(on_device, mesh=mesh, in_specs=in_specs, out_specs=out_specs, check_vma=False)
```

```python
import functools

import jax
import jax.numpy as jnp
from jax import lax
from jax.experimental import pallas as pl
from jax.experimental.pallas import tpu as pltpu
from jax.sharding import PartitionSpec as P

BLK = 128
DH = 64
CHUNK = 512
MASKED = -1e30
VMEM_LIMIT = 58 * 1024 * 1024


def contract(a, b, dims):
    return lax.dot_general(a, b, (dims, ((), ())), preferred_element_type=jnp.float32)


def row_split(block):
    lane = lax.broadcasted_iota(jnp.int32, block.shape, 1)
    zero = jnp.zeros_like(block)
    return jnp.concatenate([jnp.where(lane < DH, block, zero), jnp.where(lane >= DH, block, zero)], axis=0)


def column_split(block):
    row = lax.broadcasted_iota(jnp.int32, block.shape, 0)
    zero = jnp.zeros_like(block)
    return jnp.concatenate([jnp.where(row < DH, block, zero), jnp.where(row >= DH, block, zero)], axis=1)


def column_join(wide):
    row = lax.broadcasted_iota(jnp.int32, (wide.shape[0], BLK), 0)
    return jnp.where(row < DH, wide[:, :BLK], wide[:, BLK:])


def pair_kernel(step_rows, window, scale, turn, moved, place, bias, lo_even, lo_odd, hi_even, hi_odd,
                q_weight, o_weight, left, own, right, *rest):
    pieces, rest = rest[: len(moved)], rest[len(moved) :]
    (grads, mixed, rows_out, weights, keys, values, probs, parts, grad_out, mixed_out, x_rows, g_rows,
     through, sems_in, sems_out, sems_row, sems_piece) = rest if turn == 0 else rest[4:]
    chunks, per = window // CHUNK, CHUNK // BLK
    pair = place[turn, 0]
    even = place[turn, 1] == 0
    rim, span = left.shape[1], own.shape[1]
    for block in range(bias.shape[0]):
        start = block * step_rows

        @pl.when(pair == block)
        def _():
            taken = 0
            for source, first in ((left, 0), (own, rim), (right, rim + span)):
                lo, hi = max(start, first), min(start + window, first + source.shape[1])
                if hi > lo:
                    for half, dest in enumerate((keys, values)):
                        pltpu.make_async_copy(
                            source.at[half, pl.ds(lo - first, hi - lo)], dest.at[pl.ds(taken, hi - lo)],
                            sems_in.at[half],
                        ).start()
                    taken += hi - lo

    copies = [pltpu.make_async_copy(own.at[half], dest, sems_in.at[half]) for half, dest in enumerate((keys, values))]
    half_rows = BLK // 2

    def fetch(lo, hi):
        return [
            pltpu.make_async_copy(
                source.at[pl.ds(part * half_rows, half_rows)], dest.at[pl.ds(side * half_rows, half_rows)],
                sems_row.at[2 + 2 * part + side],
            )
            for part, dest in enumerate((x_rows, g_rows))
            for side, source in enumerate((lo, hi))
        ]

    @pl.when(even)
    def _():
        for copy in fetch(lo_even, hi_even):
            copy.start()

    @pl.when(jnp.logical_not(even))
    def _():
        for copy in fetch(lo_odd, hi_odd):
            copy.start()

    arriving = [
        pltpu.make_async_copy(piece.at[pl.ds(first, BLK)], through.at[number], sems_piece.at[0, number])
        for number, (piece, (_, first)) in enumerate(zip(pieces, moved))
    ]
    for copy in arriving:
        copy.start()
    kept = []
    for copy in fetch(lo_even, hi_even):
        copy.wait()
    out_rows = pl.ds(pl.multiple_of(pair * BLK, BLK), BLK)
    for part, source in enumerate((x_rows, g_rows)):
        copy = pltpu.make_async_copy(source, rows_out.at[part, out_rows], sems_row.at[part])
        copy.start()
        kept.append(copy)

    q = (contract(x_rows[...], q_weight[...], ((1,), (0,))) * scale).astype(jnp.bfloat16)
    grad = contract(g_rows[...], o_weight[...], ((1,), (1,))).astype(jnp.bfloat16).astype(jnp.float32)
    q_t = column_split(q.T)
    query_rows = row_split(q)
    grad_t = grad.T
    wide, tall = column_split(grad_t), row_split(grad)

    at = lambda c: slice(c * CHUNK, (c + 1) * CHUNK)
    scores = lambda c: contract(keys[at(c), :], q_t, ((1,), (0,)))
    fold = lambda t, op: op(op(t.reshape(CHUNK // 8, 8, 2 * BLK), axis=0), axis=0, keepdims=True)

    def weigh(c, half):
        parts[c] = contract(values[at(c), :].T, half, ((1,), (0,)))

    copies[0].wait()
    tops, sums = [], []
    queue, held = [scores(0), scores(1)], None
    copies[1].wait()
    for c in range(chunks):
        s = queue.pop(0)
        if c + 2 < chunks:
            queue.append(scores(c + 2))
        s = jnp.concatenate([s[j * BLK : (j + 1) * BLK] + bias[pair, c * per + j] for j in range(per)], axis=0)
        top = fold(s, jnp.max)
        e = jnp.exp(s - top)
        tops.append(top)
        sums.append(fold(e, jnp.sum))
        half = e.astype(jnp.bfloat16)
        probs[at(c), :] = half
        if held is not None:
            weigh(c - 1, held)
        held = half
    weigh(chunks - 1, held)
    tops = jnp.concatenate(tops, axis=0)
    sums = jnp.concatenate(sums, axis=0)
    f = jnp.exp(tops - jnp.max(tops, axis=0, keepdims=True))
    f = f * (1.0 / jnp.sum(f * sums, axis=0, keepdims=True))
    out = parts[0] * f[:1]
    for c in range(1, chunks):
        out = out + parts[c] * f[c : c + 1]
    attn = column_join(out).T.astype(jnp.bfloat16)
    mixed_out[:, :BLK] = attn

    product = grad_t * attn.astype(jnp.float32).T
    delta = jnp.concatenate(
        [jnp.sum(product[:DH], axis=0, keepdims=True), jnp.sum(product[DH:], axis=0, keepdims=True)], axis=1
    )
    f_t = f.T
    homes = weights.shape[0]
    for number, (by, _) in enumerate(moved):
        arriving[number].wait()
        home = lax.rem(place[turn, 2] + (by + homes), homes)
        copy = pltpu.make_async_copy(through.at[number], weights.at[home], sems_piece.at[1, number])
        copy.start()
        kept.append(copy)
    lift = lambda c: contract(values[at(c), :], (wide * f[c : c + 1]).astype(jnp.bfloat16), ((1,), (0,)))
    total = jnp.zeros((BLK, 2 * BLK), jnp.float32)
    queue = [lift(0), lift(1)]
    sent = []
    for c in range(chunks):
        dp = queue.pop(0)
        if c + 2 < chunks:
            queue.append(lift(c + 2))
        e = probs[at(c), :]
        ds = (e.astype(jnp.float32) * (dp - delta * f[c : c + 1])).astype(jnp.bfloat16)
        total = total + contract(keys[at(c), :].T, ds, ((1,), (0,)))
        grad_out[0, at(c), :] = contract(ds, query_rows, ((1,), (0,))).astype(jnp.bfloat16)
        grad_out[1, at(c), :] = contract(
            e, (tall * f_t[:, c : c + 1]).astype(jnp.bfloat16), ((1,), (0,))
        ).astype(jnp.bfloat16)
        piece = pl.ds(c * CHUNK, CHUNK)
        copy = pltpu.make_async_copy(grad_out.at[:, piece], grads.at[pair, :, piece], sems_out.at[c])
        copy.start()
        sent.append(copy)
    mixed_out[:, BLK:] = (column_join(total) * scale).T.astype(jnp.bfloat16)
    copy = pltpu.make_async_copy(mixed_out, mixed.at[out_rows], sems_row.at[6])
    copy.start()
    for copy in sent + kept + [copy]:
        copy.wait()


def terms_kernel(rows, mixed, out):
    attn = mixed[:, :BLK]
    pre = mixed[:, BLK:]
    by_query = contract(pre, rows[0], ((0,), (0,))).T.astype(jnp.bfloat16)
    by_output = contract(attn, rows[1], ((0,), (0,))).astype(jnp.bfloat16)
    count, both, _ = out.shape
    cut = both // 2
    groups = BLK // cut
    for i in range(count):
        out[i, :cut, :] = by_query[i * cut : (i + 1) * cut, :]
        row, column = (i % groups) * cut, (i // groups) * BLK
        out[i, cut:, :] = by_output[row : row + cut, column : column + BLK]


def rim_kernel(step_rows, grads, left_out, right_out, far_l, near_l, far_r, near_r, sems):
    blocks, _, window, _ = grads.shape
    rim = left_out.shape[1]
    overlap = rim - step_rows
    copies = [
        pltpu.make_async_copy(grads.at[0, :, pl.ds(0, rim)], far_l, sems.at[0]),
        pltpu.make_async_copy(grads.at[1, :, pl.ds(0, overlap)], near_l, sems.at[1]),
        pltpu.make_async_copy(grads.at[blocks - 1, :, pl.ds(window - rim, rim)], far_r, sems.at[2]),
        pltpu.make_async_copy(grads.at[blocks - 2, :, pl.ds(window - overlap, overlap)], near_r, sems.at[3]),
    ]
    for copy in copies:
        copy.start()
    for copy in copies:
        copy.wait()
    add = lambda a, b: (a.astype(jnp.float32) + b.astype(jnp.float32)).astype(jnp.bfloat16)
    left_out[:, :step_rows, :] = far_l[:, :step_rows, :]
    left_out[:, step_rows:, :] = add(far_l[:, step_rows:, :], near_l[...])
    right_out[:, :overlap, :] = add(far_r[:, :overlap, :], near_r[...])
    right_out[:, overlap:, :] = far_r[:, overlap:, :]


def combine_kernel(step_rows, grads, from_left, from_right, out, held, result, sems, sems_out):
    blocks, _, window, _ = grads.shape
    rows, rim = out.shape[1], from_left.shape[1]
    plan = []
    slot = 0
    for first in range(0, rows, CHUNK):
        sources = []
        for block in range(blocks):
            local = first + rim - block * step_rows
            if 0 <= local < window:
                sources.append((grads.at[block, :, pl.ds(local, CHUNK)], slot))
                slot += 1
        if first < rim:
            sources.append((from_left.at[:, pl.ds(first, CHUNK)], slot))
            slot += 1
        if first >= rows - rim:
            sources.append((from_right.at[:, pl.ds(first - (rows - rim), CHUNK)], slot))
            slot += 1
        copies = [pltpu.make_async_copy(source, held.at[n], sems.at[n]) for source, n in sources]
        for copy in copies:
            copy.start()
        plan.append((first, sources, copies))
    sent = []
    for number, (first, sources, copies) in enumerate(plan):
        for copy in copies:
            copy.wait()
        part = held[sources[0][1]].astype(jnp.float32)
        for _, n in sources[1:]:
            part = part + held[n].astype(jnp.float32)
        result[:, first : first + CHUNK, :] = part.astype(jnp.bfloat16)
        piece = pl.ds(first, CHUNK)
        copy = pltpu.make_async_copy(result.at[:, piece], out.at[:, piece], sems_out.at[number])
        copy.start()
        sent.append(copy)
    for copy in sent:
        copy.wait()


ANYWHERE = pl.BlockSpec(memory_space=pl.ANY)
IN_VMEM = pl.BlockSpec(memory_space=pltpu.VMEM)
IN_SMEM = pl.BlockSpec(memory_space=pltpu.SMEM)


def params():
    return pltpu.CompilerParams(vmem_limit_bytes=VMEM_LIMIT)


def cost(flops, moved, exps=0):
    return pl.CostEstimate(flops=flops, bytes_accessed=moved, transcendentals=exps)


def pack_kernel(flag, x, g, o_weight, q_weight, kv, out, tail, head, sems):
    rows = x.shape[0]
    span, rim = kv.shape[1], tail.shape[1]
    copies = [
        pltpu.make_async_copy(kv.at[:, pl.ds(span - rim, rim)], tail, sems.at[0]),
        pltpu.make_async_copy(kv.at[:, pl.ds(0, rim)], head, sems.at[1]),
    ]
    for copy in copies:
        copy.start()
    out[:rows, :] = x[...]
    out[rows : 2 * rows, :] = g[...]

    @pl.when(flag[0] == 0)
    def _():
        out[2 * rows :, :] = o_weight[...]

    @pl.when(flag[0] != 0)
    def _():
        out[2 * rows :, :] = q_weight[...].T

    for copy in copies:
        copy.wait()


def pack(flag, x, g, o_weight, q_weight, kv, rim):
    edge = jax.ShapeDtypeStruct((2, rim, BLK), kv.dtype)
    return pl.pallas_call(
        pack_kernel,
        in_specs=[IN_SMEM] + [IN_VMEM] * 4 + [ANYWHERE],
        out_specs=[IN_VMEM] * 3,
        out_shape=[jax.ShapeDtypeStruct((2 * x.shape[0] + o_weight.shape[0], x.shape[1]), x.dtype), edge, edge],
        scratch_shapes=[pltpu.SemaphoreType.DMA((2,))],
        cost_estimate=cost(0, 4_000_000),
        name="pack",
    )(flag, x, g, o_weight, q_weight, kv)


def attention_pair(turn, place, bias, shards, moved, q_weight, o_weight, left, own, right, carried, blocks, homes,
                   step_rows, window):
    width = q_weight.shape[0]
    chunks = window // CHUNK
    shapes = [
        jax.ShapeDtypeStruct((blocks, 2, window, BLK), jnp.bfloat16),
        jax.ShapeDtypeStruct((blocks * BLK, 2 * BLK), jnp.bfloat16),
        jax.ShapeDtypeStruct((2, blocks * BLK, width), jnp.bfloat16),
        jax.ShapeDtypeStruct((homes, BLK, width), jnp.bfloat16),
    ]
    extra = () if carried is None else tuple(carried)
    pieces = [piece for piece, _, _ in moved]
    first_extra = 11 + len(pieces)
    bf = lambda *shape: pltpu.VMEM(shape, jnp.bfloat16)
    return pl.pallas_call(
        functools.partial(pair_kernel, step_rows, window, DH ** -0.5, turn, [m[1:] for m in moved]),
        in_specs=[IN_SMEM, IN_SMEM] + [ANYWHERE] * 4 + [IN_VMEM] * 2 + [ANYWHERE] * (3 + len(pieces) + len(extra)),
        out_specs=[ANYWHERE] * 4,
        out_shape=shapes,
        input_output_aliases={first_extra + i: i for i in range(len(extra))},
        scratch_shapes=[
            bf(window, BLK), bf(window, BLK),
            bf(window, 2 * BLK), pltpu.VMEM((chunks, BLK, 2 * BLK), jnp.float32),
            bf(2, window, BLK), bf(BLK, 2 * BLK), bf(BLK, width), bf(BLK, width), bf(len(pieces), BLK, width),
            pltpu.SemaphoreType.DMA((2,)), pltpu.SemaphoreType.DMA((chunks,)), pltpu.SemaphoreType.DMA((7,)),
            pltpu.SemaphoreType.DMA((2, len(pieces))),
        ],
        compiler_params=params(),
        cost_estimate=cost(4_000_000_000, 10_000_000, window * 2 * BLK),
        name="attention_pair",
    )(place, bias, *shards, q_weight, o_weight, left, own, right, *pieces, *extra)


def weight_terms(rows, mixed, parts):
    width = rows.shape[2]
    return pl.pallas_call(
        terms_kernel,
        in_specs=[IN_VMEM] * 2,
        out_specs=IN_VMEM,
        out_shape=jax.ShapeDtypeStruct((parts, 2 * width // parts, BLK), jnp.bfloat16),
        compiler_params=params(),
        cost_estimate=cost(1_000_000_000, 4_000_000),
        name="weight_terms",
    )(rows, mixed)


def rim_grads(grads, rim, step_rows):
    bf = lambda rows: pltpu.VMEM((2, rows, BLK), jnp.bfloat16)
    edge = jax.ShapeDtypeStruct((2, rim, BLK), jnp.bfloat16)
    return pl.pallas_call(
        functools.partial(rim_kernel, step_rows),
        in_specs=[ANYWHERE],
        out_specs=[IN_VMEM] * 2,
        out_shape=[edge, edge],
        scratch_shapes=[bf(rim), bf(rim - step_rows), bf(rim), bf(rim - step_rows), pltpu.SemaphoreType.DMA((4,))],
        compiler_params=params(),
        cost_estimate=cost(1_000_000, 5_000_000),
        name="rim_grads",
    )(grads)


def combine_grads(grads, from_left, from_right, rows, step_rows):
    blocks, _, window, _ = grads.shape
    rim = from_left.shape[1]
    inside = sum(
        0 <= first + rim - block * step_rows < window for first in range(0, rows, CHUNK) for block in range(blocks)
    )
    slots = inside + 2 * (rim // CHUNK)
    return pl.pallas_call(
        functools.partial(combine_kernel, step_rows),
        in_specs=[ANYWHERE] * 3,
        out_specs=ANYWHERE,
        out_shape=jax.ShapeDtypeStruct((2, rows, BLK), jnp.bfloat16),
        scratch_shapes=[
            pltpu.VMEM((slots, 2, CHUNK, BLK), jnp.bfloat16),
            pltpu.VMEM((2, rows, BLK), jnp.bfloat16),
            pltpu.SemaphoreType.DMA((slots,)),
            pltpu.SemaphoreType.DMA((rows // CHUNK,)),
        ],
        compiler_params=params(),
        cost_estimate=cost(5_000_000, 10_000_000),
        name="combine_grads",
    )(grads, from_left, from_right)


def shifted(count, by):
    return [(i, (i + by) % count) for i in range(count)]


def band_bias(band_lists, base_block, query_blocks, half_step, reach_blocks):
    local = jnp.arange(query_blocks, dtype=jnp.int32)
    window_first = base_block + (2 * local + 1) * half_step - reach_blocks
    wanted = window_first[:, None] + jnp.arange(2 * reach_blocks, dtype=jnp.int32)[None, :]
    allowed = jnp.any(band_lists[:, :, None] == wanted[:, None, :], axis=1)
    return jnp.where(allowed, 0.0, MASKED).astype(jnp.float32)


def added(arrived):
    return jnp.sum(arrived.astype(jnp.float32), axis=0, keepdims=True).astype(jnp.bfloat16)


def exchange(parts, axis):
    return lax.all_to_all(parts, axis, 0, 0, tiled=True)


def on_device(slow_x, q_weight, o_weight, fast_kv, mask_lists, cotangent):
    own_rows, width = slow_x.shape
    tp = lax.axis_size("tp")
    ctx = lax.axis_size("ctx")
    total_rows = own_rows * tp
    query_blocks = total_rows // BLK
    fast_rows = fast_kv.shape[1]
    fast_blocks = fast_rows // BLK
    half_step = fast_blocks // (2 * query_blocks)
    reach_blocks = mask_lists.shape[1] // 2
    rim = (reach_blocks - half_step) * BLK
    window = 2 * reach_blocks * BLK
    step_rows = 2 * half_step * BLK

    ctx_index = lax.axis_index("ctx")
    flag = (ctx_index % 2).reshape(1).astype(jnp.int32)
    own, tail, head = pack(flag, slow_x, cotangent, o_weight, q_weight, fast_kv, rim)
    up = [(i, i + 1) for i in range(ctx - 1)]
    down = [(i + 1, i) for i in range(ctx - 1)]
    left = lax.ppermute(tail, "ctx", up)
    right = lax.ppermute(head, "ctx", down)

    even = ctx_index % 2 == 0
    band_lists = lax.dynamic_slice_in_dim(mask_lists, ctx_index * query_blocks, query_blocks, 0)
    bias = band_bias(band_lists, ctx_index * fast_blocks, query_blocks, half_step, reach_blocks)
    tp_index = lax.axis_index("tp")
    parity = tp_index % 2
    turn = 1 - 2 * parity
    middle = tp_index // 2
    moves = jnp.array([0, 0, 0, 2], jnp.int32) + jnp.array([0, -1, 1, 0], jnp.int32) * turn
    pairs = (middle + moves + query_blocks) % query_blocks
    spread = lambda value: jnp.broadcast_to(value, pairs.shape)
    place = jnp.stack([pairs, spread(parity), spread(tp_index)], axis=1).astype(jnp.int32)
    ahead, behind = shifted(tp, 1), shifted(tp, -1)
    shared = 2 * own_rows
    f, b = [own], [own]

    def pass_on(gate):
        back, front = f[-1], b[-1]
        if gate is not None:
            back, front, gate = lax.optimization_barrier((back, front, gate))
        if 2 * len(f) < tp:
            f.append(lax.ppermute(back, "tp", ahead))
            b.append(lax.ppermute(front, "tp", behind))
        else:
            f.append(lax.ppermute(back[:shared], "tp", ahead))
            b.append(lax.ppermute(front[shared:], "tp", behind))
        return gate

    picks = [
        lambda: ((own, f[1], b[1], own), [(own, 0, shared), (f[1], -1, shared), (b[1], 1, shared)]),
        lambda: ((f[2], b[1], f[1], b[2]), [(f[2], -2, shared), (b[2], 2, shared)]),
        lambda: ((b[2], f[3], b[3], f[2]), [(f[3], -3, shared), (b[3], 3, shared)]),
        lambda: ((f[4], b[3], f[3], f[4]), [(b[4], 4, 0)]),
    ]
    pass_on(None)
    pass_on(None)
    carried = None
    for number, pick in enumerate(picks):
        shards, moved = pick()
        carried = attention_pair(
            number, place, bias, shards, moved, q_weight, o_weight, left, fast_kv, right, carried, query_blocks, tp,
            step_rows, window,
        )
        if len(f) <= tp // 2:
            carried = (carried[0], pass_on(carried[1])) + tuple(carried[2:])
    grads, rows_mixed, rows_all, mine = carried

    mixed = exchange(rows_mixed.reshape(tp, own_rows, 2 * BLK), "tp")
    left_grads, right_grads = rim_grads(grads, rim, step_rows)
    rows_all, left_grads, right_grads = lax.optimization_barrier((rows_all, left_grads, right_grads))
    terms = weight_terms(rows_all, rows_mixed, ctx)
    terms, mixed = lax.optimization_barrier((terms, mixed))
    own_terms = added(exchange(terms, "ctx"))
    from_right = lax.ppermute(left_grads, "ctx", down)
    from_left = lax.ppermute(right_grads, "ctx", up)
    other = lax.ppermute(mine, "ctx", [(i, i ^ 1) for i in range(ctx)])
    summed = exchange(jnp.broadcast_to(own_terms, terms.shape), "ctx")
    grad_kv = combine_grads(grads, from_left, from_right, fast_rows, step_rows)

    first = jnp.where(even, mixed[:, :, :BLK], mixed[:, :, BLK:])
    second = jnp.where(even, mixed[:, :, BLK:], mixed[:, :, :BLK])
    project = lambda rows, full: jnp.einsum(
        "trk,tkn->rn", rows, full.reshape(tp, BLK, width), preferred_element_type=jnp.float32
    ).astype(jnp.bfloat16)
    first = project(first, mine)
    second = project(second, other)
    attended = jnp.where(even, first, second)
    grad_slow = jnp.where(even, second, first)

    summed, attended, grad_slow, grad_kv = lax.optimization_barrier((summed, attended, grad_slow, grad_kv))
    cut = terms.shape[1] // 2
    grad_q_weight = summed[:, :cut].astype(jnp.float32).reshape(q_weight.shape)
    blocked = summed[:, cut:].reshape(width // BLK, BLK // cut, cut, BLK).transpose(1, 2, 0, 3)
    grad_o_weight = blocked.astype(jnp.float32).reshape(o_weight.shape)
    return (attended, grad_slow, grad_q_weight, grad_o_weight, grad_kv)


def solution(mesh):
    in_specs = (
        P(("ctx", "tp"), None),
        P(None, "tp"),
        P("tp", None),
        P(None, "ctx", "tp"),
        P(),
        P(("ctx", "tp"), None),
    )
    out_specs = (
        P(("ctx", "tp"), None),
        P(("ctx", "tp"), None),
        P(None, "tp"),
        P("tp", None),
        P(None, "ctx", "tp"),
    )
    return jax.shard_map(on_device, mesh=mesh, in_specs=in_specs, out_specs=out_specs, check_vma=False)
```

```python
import functools

import jax
import jax.numpy as jnp
from jax import lax
from jax.experimental import pallas as pl
from jax.experimental.pallas import tpu as pltpu
from jax.sharding import PartitionSpec as P

BLK = 128
DH = 64
CHUNK = 512
MASKED = -1e30
VMEM_LIMIT = 58 * 1024 * 1024


def contract(a, b, dims):
    return lax.dot_general(a, b, (dims, ((), ())), preferred_element_type=jnp.float32)


def row_split(block):
    lane = lax.broadcasted_iota(jnp.int32, block.shape, 1)
    zero = jnp.zeros_like(block)
    return jnp.concatenate([jnp.where(lane < DH, block, zero), jnp.where(lane >= DH, block, zero)], axis=0)


def column_split(block):
    row = lax.broadcasted_iota(jnp.int32, block.shape, 0)
    zero = jnp.zeros_like(block)
    return jnp.concatenate([jnp.where(row < DH, block, zero), jnp.where(row >= DH, block, zero)], axis=1)


def column_join(wide):
    row = lax.broadcasted_iota(jnp.int32, (wide.shape[0], BLK), 0)
    return jnp.where(row < DH, wide[:, :BLK], wide[:, BLK:])


def pair_kernel(step_rows, window, scale, turn, moved, place, bias, lo_even, lo_odd, hi_even, hi_odd,
                q_weight, o_weight, left, own, right, *rest):
    pieces, rest = rest[: len(moved)], rest[len(moved) :]
    (grads, mixed, rows_out, weights, keys, values, probs, parts, grad_out, mixed_out, x_rows, g_rows,
     through, sems_in, sems_out, sems_row, sems_piece) = rest if turn == 0 else rest[4:]
    chunks, per = window // CHUNK, CHUNK // BLK
    pair = place[turn, 0]
    even = place[turn, 1] == 0
    rim, span = left.shape[1], own.shape[1]
    for block in range(bias.shape[0]):
        start = block * step_rows

        @pl.when(pair == block)
        def _():
            taken = 0
            for source, first in ((left, 0), (own, rim), (right, rim + span)):
                lo, hi = max(start, first), min(start + window, first + source.shape[1])
                if hi > lo:
                    for half, dest in enumerate((keys, values)):
                        pltpu.make_async_copy(
                            source.at[half, pl.ds(lo - first, hi - lo)], dest.at[pl.ds(taken, hi - lo)],
                            sems_in.at[half],
                        ).start()
                    taken += hi - lo

    copies = [pltpu.make_async_copy(own.at[half], dest, sems_in.at[half]) for half, dest in enumerate((keys, values))]
    half_rows = BLK // 2

    def fetch(lo, hi):
        return [
            pltpu.make_async_copy(
                source.at[pl.ds(part * half_rows, half_rows)], dest.at[pl.ds(side * half_rows, half_rows)],
                sems_row.at[2 + 2 * part + side],
            )
            for part, dest in enumerate((x_rows, g_rows))
            for side, source in enumerate((lo, hi))
        ]

    @pl.when(even)
    def _():
        for copy in fetch(lo_even, hi_even):
            copy.start()

    @pl.when(jnp.logical_not(even))
    def _():
        for copy in fetch(lo_odd, hi_odd):
            copy.start()

    arriving = [
        pltpu.make_async_copy(piece.at[pl.ds(first, BLK)], through.at[number], sems_piece.at[0, number])
        for number, (piece, (_, first)) in enumerate(zip(pieces, moved))
    ]
    for copy in arriving:
        copy.start()
    kept = []
    for copy in fetch(lo_even, hi_even):
        copy.wait()
    out_rows = pl.ds(pl.multiple_of(pair * BLK, BLK), BLK)
    for part, source in enumerate((x_rows, g_rows)):
        copy = pltpu.make_async_copy(source, rows_out.at[part, out_rows], sems_row.at[part])
        copy.start()
        kept.append(copy)

    q = (contract(x_rows[...], q_weight[...], ((1,), (0,))) * scale).astype(jnp.bfloat16)
    grad = contract(g_rows[...], o_weight[...], ((1,), (1,))).astype(jnp.bfloat16).astype(jnp.float32)
    q_t = column_split(q.T)
    query_rows = row_split(q)
    grad_t = grad.T
    wide, tall = column_split(grad_t), row_split(grad)

    at = lambda c: slice(c * CHUNK, (c + 1) * CHUNK)
    scores = lambda c: contract(keys[at(c), :], q_t, ((1,), (0,)))
    fold = lambda t, op: op(op(t.reshape(CHUNK // 8, 8, 2 * BLK), axis=0), axis=0, keepdims=True)

    def weigh(c, half):
        parts[c] = contract(values[at(c), :].T, half, ((1,), (0,)))

    copies[0].wait()
    tops, sums = [], []
    queue, held = [scores(0), scores(1)], None
    copies[1].wait()
    for c in range(chunks):
        s = queue.pop(0)
        if c + 2 < chunks:
            queue.append(scores(c + 2))
        s = jnp.concatenate([s[j * BLK : (j + 1) * BLK] + bias[pair, c * per + j] for j in range(per)], axis=0)
        top = fold(s, jnp.max)
        e = jnp.exp(s - top)
        tops.append(top)
        sums.append(fold(e, jnp.sum))
        half = e.astype(jnp.bfloat16)
        probs[at(c), :] = half
        if held is not None:
            weigh(c - 1, held)
        held = half
    weigh(chunks - 1, held)
    tops = jnp.concatenate(tops, axis=0)
    sums = jnp.concatenate(sums, axis=0)
    f = jnp.exp(tops - jnp.max(tops, axis=0, keepdims=True))
    f = f * (1.0 / jnp.sum(f * sums, axis=0, keepdims=True))
    out = parts[0] * f[:1]
    for c in range(1, chunks):
        out = out + parts[c] * f[c : c + 1]
    attn = column_join(out).T.astype(jnp.bfloat16)
    mixed_out[:, :BLK] = attn

    product = grad_t * attn.astype(jnp.float32).T
    delta = jnp.concatenate(
        [jnp.sum(product[:DH], axis=0, keepdims=True), jnp.sum(product[DH:], axis=0, keepdims=True)], axis=1
    )
    f_t = f.T
    homes = weights.shape[0]
    for number, (by, _) in enumerate(moved):
        arriving[number].wait()
        home = lax.rem(place[turn, 2] + (by + homes), homes)
        copy = pltpu.make_async_copy(through.at[number], weights.at[home], sems_piece.at[1, number])
        copy.start()
        kept.append(copy)
    lift = lambda c: contract(values[at(c), :], (wide * f[c : c + 1]).astype(jnp.bfloat16), ((1,), (0,)))
    total = jnp.zeros((BLK, 2 * BLK), jnp.float32)
    queue = [lift(0), lift(1)]
    sent = []
    for c in range(chunks):
        dp = queue.pop(0)
        if c + 2 < chunks:
            queue.append(lift(c + 2))
        e = probs[at(c), :]
        ds = (e.astype(jnp.float32) * (dp - delta * f[c : c + 1])).astype(jnp.bfloat16)
        total = total + contract(keys[at(c), :].T, ds, ((1,), (0,)))
        grad_out[0, at(c), :] = contract(ds, query_rows, ((1,), (0,))).astype(jnp.bfloat16)
        grad_out[1, at(c), :] = contract(
            e, (tall * f_t[:, c : c + 1]).astype(jnp.bfloat16), ((1,), (0,))
        ).astype(jnp.bfloat16)
        piece = pl.ds(c * CHUNK, CHUNK)
        copy = pltpu.make_async_copy(grad_out.at[:, piece], grads.at[pair, :, piece], sems_out.at[c])
        copy.start()
        sent.append(copy)
    mixed_out[:, BLK:] = (column_join(total) * scale).T.astype(jnp.bfloat16)
    copy = pltpu.make_async_copy(mixed_out, mixed.at[out_rows], sems_row.at[6])
    copy.start()
    for copy in sent + kept + [copy]:
        copy.wait()


def terms_kernel(flag, rows, mixed, keep, send):
    by_query = contract(mixed[:, BLK:], rows[0], ((0,), (0,))).T.astype(jnp.bfloat16)
    by_output = contract(mixed[:, :BLK], rows[1], ((0,), (0,))).astype(jnp.bfloat16)
    count, cut, _ = keep.shape
    groups = BLK // cut

    def store(q_out, o_out):
        for i in range(count):
            q_out[i] = by_query[i * cut : (i + 1) * cut, :]
            row, column = (i % groups) * cut, (i // groups) * BLK
            o_out[i] = by_output[row : row + cut, column : column + BLK]

    @pl.when(flag[0] == 0)
    def _():
        store(keep, send)

    @pl.when(flag[0] != 0)
    def _():
        store(send, keep)


def rim_kernel(step_rows, grads, left_out, right_out, far_l, near_l, far_r, near_r, sems):
    blocks, _, window, _ = grads.shape
    rim = left_out.shape[1]
    overlap = rim - step_rows
    copies = [
        pltpu.make_async_copy(grads.at[0, :, pl.ds(0, rim)], far_l, sems.at[0]),
        pltpu.make_async_copy(grads.at[1, :, pl.ds(0, overlap)], near_l, sems.at[1]),
        pltpu.make_async_copy(grads.at[blocks - 1, :, pl.ds(window - rim, rim)], far_r, sems.at[2]),
        pltpu.make_async_copy(grads.at[blocks - 2, :, pl.ds(window - overlap, overlap)], near_r, sems.at[3]),
    ]
    for copy in copies:
        copy.start()
    for copy in copies:
        copy.wait()
    add = lambda a, b: (a.astype(jnp.float32) + b.astype(jnp.float32)).astype(jnp.bfloat16)
    left_out[:, :step_rows, :] = far_l[:, :step_rows, :]
    left_out[:, step_rows:, :] = add(far_l[:, step_rows:, :], near_l[...])
    right_out[:, :overlap, :] = add(far_r[:, :overlap, :], near_r[...])
    right_out[:, overlap:, :] = far_r[:, overlap:, :]


def combine_kernel(step_rows, grads, from_left, from_right, out, held, result, sems, sems_out):
    blocks, _, window, _ = grads.shape
    rows, rim = out.shape[1], from_left.shape[1]
    plan = []
    slot = 0
    for first in range(0, rows, CHUNK):
        sources = []
        for block in range(blocks):
            local = first + rim - block * step_rows
            if 0 <= local < window:
                sources.append((grads.at[block, :, pl.ds(local, CHUNK)], slot))
                slot += 1
        if first < rim:
            sources.append((from_left.at[:, pl.ds(first, CHUNK)], slot))
            slot += 1
        if first >= rows - rim:
            sources.append((from_right.at[:, pl.ds(first - (rows - rim), CHUNK)], slot))
            slot += 1
        copies = [pltpu.make_async_copy(source, held.at[n], sems.at[n]) for source, n in sources]
        for copy in copies:
            copy.start()
        plan.append((first, sources, copies))
    sent = []
    for number, (first, sources, copies) in enumerate(plan):
        for copy in copies:
            copy.wait()
        part = held[sources[0][1]].astype(jnp.float32)
        for _, n in sources[1:]:
            part = part + held[n].astype(jnp.float32)
        result[:, first : first + CHUNK, :] = part.astype(jnp.bfloat16)
        piece = pl.ds(first, CHUNK)
        copy = pltpu.make_async_copy(result.at[:, piece], out.at[:, piece], sems_out.at[number])
        copy.start()
        sent.append(copy)
    for copy in sent:
        copy.wait()


ANYWHERE = pl.BlockSpec(memory_space=pl.ANY)
IN_VMEM = pl.BlockSpec(memory_space=pltpu.VMEM)
IN_SMEM = pl.BlockSpec(memory_space=pltpu.SMEM)


def params():
    return pltpu.CompilerParams(vmem_limit_bytes=VMEM_LIMIT)


def cost(flops, moved, exps=0):
    return pl.CostEstimate(flops=flops, bytes_accessed=moved, transcendentals=exps)


def pack_kernel(flag, x, g, o_weight, q_weight, kv, out, tail, head, sems):
    rows = x.shape[0]
    span, rim = kv.shape[1], tail.shape[1]
    copies = [
        pltpu.make_async_copy(kv.at[:, pl.ds(span - rim, rim)], tail, sems.at[0]),
        pltpu.make_async_copy(kv.at[:, pl.ds(0, rim)], head, sems.at[1]),
    ]
    for copy in copies:
        copy.start()
    out[:rows, :] = x[...]
    out[rows : 2 * rows, :] = g[...]

    @pl.when(flag[0] == 0)
    def _():
        out[2 * rows :, :] = o_weight[...]

    @pl.when(flag[0] != 0)
    def _():
        out[2 * rows :, :] = q_weight[...].T

    for copy in copies:
        copy.wait()


def pack(flag, x, g, o_weight, q_weight, kv, rim):
    edge = jax.ShapeDtypeStruct((2, rim, BLK), kv.dtype)
    return pl.pallas_call(
        pack_kernel,
        in_specs=[IN_SMEM] + [IN_VMEM] * 4 + [ANYWHERE],
        out_specs=[IN_VMEM] * 3,
        out_shape=[jax.ShapeDtypeStruct((2 * x.shape[0] + o_weight.shape[0], x.shape[1]), x.dtype), edge, edge],
        scratch_shapes=[pltpu.SemaphoreType.DMA((2,))],
        cost_estimate=cost(0, 4_000_000),
        name="pack",
    )(flag, x, g, o_weight, q_weight, kv)


def attention_pair(turn, place, bias, shards, moved, q_weight, o_weight, left, own, right, carried, blocks, homes,
                   step_rows, window):
    width = q_weight.shape[0]
    chunks = window // CHUNK
    shapes = [
        jax.ShapeDtypeStruct((blocks, 2, window, BLK), jnp.bfloat16),
        jax.ShapeDtypeStruct((blocks * BLK, 2 * BLK), jnp.bfloat16),
        jax.ShapeDtypeStruct((2, blocks * BLK, width), jnp.bfloat16),
        jax.ShapeDtypeStruct((homes, BLK, width), jnp.bfloat16),
    ]
    extra = () if carried is None else tuple(carried)
    pieces = [piece for piece, _, _ in moved]
    first_extra = 11 + len(pieces)
    bf = lambda *shape: pltpu.VMEM(shape, jnp.bfloat16)
    return pl.pallas_call(
        functools.partial(pair_kernel, step_rows, window, DH ** -0.5, turn, [m[1:] for m in moved]),
        in_specs=[IN_SMEM, IN_SMEM] + [ANYWHERE] * 4 + [IN_VMEM] * 2 + [ANYWHERE] * (3 + len(pieces) + len(extra)),
        out_specs=[ANYWHERE] * 4,
        out_shape=shapes,
        input_output_aliases={first_extra + i: i for i in range(len(extra))},
        scratch_shapes=[
            bf(window, BLK), bf(window, BLK),
            bf(window, 2 * BLK), pltpu.VMEM((chunks, BLK, 2 * BLK), jnp.float32),
            bf(2, window, BLK), bf(BLK, 2 * BLK), bf(BLK, width), bf(BLK, width), bf(len(pieces), BLK, width),
            pltpu.SemaphoreType.DMA((2,)), pltpu.SemaphoreType.DMA((chunks,)), pltpu.SemaphoreType.DMA((7,)),
            pltpu.SemaphoreType.DMA((2, len(pieces))),
        ],
        compiler_params=params(),
        cost_estimate=cost(4_000_000_000, 10_000_000, window * 2 * BLK),
        name="attention_pair",
    )(place, bias, *shards, q_weight, o_weight, left, own, right, *pieces, *extra)


def weight_terms(flag, rows, mixed, parts):
    half = jax.ShapeDtypeStruct((parts, rows.shape[2] // parts, BLK), jnp.bfloat16)
    return pl.pallas_call(
        terms_kernel,
        in_specs=[IN_SMEM] + [IN_VMEM] * 2,
        out_specs=[IN_VMEM] * 2,
        out_shape=[half, half],
        compiler_params=params(),
        cost_estimate=cost(1_000_000_000, 4_000_000),
        name="weight_terms",
    )(flag, rows, mixed)


def rim_grads(grads, rim, step_rows):
    bf = lambda rows: pltpu.VMEM((2, rows, BLK), jnp.bfloat16)
    edge = jax.ShapeDtypeStruct((2, rim, BLK), jnp.bfloat16)
    return pl.pallas_call(
        functools.partial(rim_kernel, step_rows),
        in_specs=[ANYWHERE],
        out_specs=[IN_VMEM] * 2,
        out_shape=[edge, edge],
        scratch_shapes=[bf(rim), bf(rim - step_rows), bf(rim), bf(rim - step_rows), pltpu.SemaphoreType.DMA((4,))],
        compiler_params=params(),
        cost_estimate=cost(1_000_000, 5_000_000),
        name="rim_grads",
    )(grads)


def combine_grads(grads, from_left, from_right, rows, step_rows):
    blocks, _, window, _ = grads.shape
    rim = from_left.shape[1]
    inside = sum(
        0 <= first + rim - block * step_rows < window for first in range(0, rows, CHUNK) for block in range(blocks)
    )
    slots = inside + 2 * (rim // CHUNK)
    return pl.pallas_call(
        functools.partial(combine_kernel, step_rows),
        in_specs=[ANYWHERE] * 3,
        out_specs=ANYWHERE,
        out_shape=jax.ShapeDtypeStruct((2, rows, BLK), jnp.bfloat16),
        scratch_shapes=[
            pltpu.VMEM((slots, 2, CHUNK, BLK), jnp.bfloat16),
            pltpu.VMEM((2, rows, BLK), jnp.bfloat16),
            pltpu.SemaphoreType.DMA((slots,)),
            pltpu.SemaphoreType.DMA((rows // CHUNK,)),
        ],
        compiler_params=params(),
        cost_estimate=cost(5_000_000, 10_000_000),
        name="combine_grads",
    )(grads, from_left, from_right)


def shifted(count, by):
    return [(i, (i + by) % count) for i in range(count)]


def band_bias(band_lists, base_block, query_blocks, half_step, reach_blocks):
    local = jnp.arange(query_blocks, dtype=jnp.int32)
    window_first = base_block + (2 * local + 1) * half_step - reach_blocks
    wanted = window_first[:, None] + jnp.arange(2 * reach_blocks, dtype=jnp.int32)[None, :]
    allowed = jnp.any(band_lists[:, :, None] == wanted[:, None, :], axis=1)
    return jnp.where(allowed, 0.0, MASKED).astype(jnp.float32)


def added(arrived):
    return jnp.sum(arrived.astype(jnp.float32), axis=0, keepdims=True).astype(jnp.bfloat16)


def exchange(parts, axis, groups=None):
    return lax.all_to_all(parts, axis, 0, 0, tiled=True, axis_index_groups=groups)


def on_device(slow_x, q_weight, o_weight, fast_kv, mask_lists, cotangent):
    own_rows, width = slow_x.shape
    tp = lax.axis_size("tp")
    ctx = lax.axis_size("ctx")
    total_rows = own_rows * tp
    query_blocks = total_rows // BLK
    fast_rows = fast_kv.shape[1]
    fast_blocks = fast_rows // BLK
    half_step = fast_blocks // (2 * query_blocks)
    reach_blocks = mask_lists.shape[1] // 2
    rim = (reach_blocks - half_step) * BLK
    window = 2 * reach_blocks * BLK
    step_rows = 2 * half_step * BLK

    ctx_index = lax.axis_index("ctx")
    flag = (ctx_index % 2).reshape(1).astype(jnp.int32)
    own, tail, head = pack(flag, slow_x, cotangent, o_weight, q_weight, fast_kv, rim)
    up = [(i, i + 1) for i in range(ctx - 1)]
    down = [(i + 1, i) for i in range(ctx - 1)]
    left = lax.ppermute(tail, "ctx", up)
    right = lax.ppermute(head, "ctx", down)

    even = ctx_index % 2 == 0
    band_lists = lax.dynamic_slice_in_dim(mask_lists, ctx_index * query_blocks, query_blocks, 0)
    bias = band_bias(band_lists, ctx_index * fast_blocks, query_blocks, half_step, reach_blocks)
    tp_index = lax.axis_index("tp")
    parity = tp_index % 2
    turn = 1 - 2 * parity
    middle = tp_index // 2
    moves = jnp.array([0, 0, 0, 2], jnp.int32) + jnp.array([0, -1, 1, 0], jnp.int32) * turn
    pairs = (middle + moves + query_blocks) % query_blocks
    spread = lambda value: jnp.broadcast_to(value, pairs.shape)
    place = jnp.stack([pairs, spread(parity), spread(tp_index)], axis=1).astype(jnp.int32)
    ahead, behind = shifted(tp, 1), shifted(tp, -1)
    shared = 2 * own_rows
    f, b = [own], [own]

    def pass_on(gate):
        back, front = f[-1], b[-1]
        if gate is not None:
            back, front, gate = lax.optimization_barrier((back, front, gate))
        if 2 * len(f) < tp:
            f.append(lax.ppermute(back, "tp", ahead))
            b.append(lax.ppermute(front, "tp", behind))
        else:
            f.append(lax.ppermute(back[:shared], "tp", ahead))
            b.append(lax.ppermute(front[shared:], "tp", behind))
        return gate

    picks = [
        lambda: ((own, f[1], b[1], own), [(own, 0, shared), (f[1], -1, shared), (b[1], 1, shared)]),
        lambda: ((f[2], b[1], f[1], b[2]), [(f[2], -2, shared), (b[2], 2, shared)]),
        lambda: ((b[2], f[3], b[3], f[2]), [(f[3], -3, shared), (b[3], 3, shared)]),
        lambda: ((f[4], b[3], f[3], f[4]), [(b[4], 4, 0)]),
    ]
    pass_on(None)
    pass_on(None)
    carried = None
    for number, pick in enumerate(picks):
        shards, moved = pick()
        carried = attention_pair(
            number, place, bias, shards, moved, q_weight, o_weight, left, fast_kv, right, carried, query_blocks, tp,
            step_rows, window,
        )
        if len(f) <= tp // 2:
            carried = (carried[0], pass_on(carried[1])) + tuple(carried[2:])
    grads, rows_mixed, rows_all, mine = carried

    mixed = exchange(rows_mixed.reshape(tp, own_rows, 2 * BLK), "tp")
    left_grads, right_grads = rim_grads(grads, rim, step_rows)
    rows_all, left_grads, right_grads = lax.optimization_barrier((rows_all, left_grads, right_grads))
    keep, send = weight_terms(flag, rows_all, rows_mixed, ctx)
    swap = [(i, i ^ 1) for i in range(ctx)]
    groups = [list(range(side, ctx, 2)) for side in range(2)]
    partner = lax.ppermute(send, "ctx", swap)
    keep, mixed = lax.optimization_barrier((keep, mixed))
    terms = (keep.astype(jnp.float32) + partner.astype(jnp.float32)).astype(jnp.bfloat16)
    terms = terms.reshape(ctx // 2, -1, BLK)
    own_terms = added(exchange(terms, "ctx", groups))
    from_right = lax.ppermute(left_grads, "ctx", down)
    from_left = lax.ppermute(right_grads, "ctx", up)
    other = lax.ppermute(mine, "ctx", [(i, i ^ 1) for i in range(ctx)])
    summed = exchange(jnp.broadcast_to(own_terms, terms.shape), "ctx", groups)
    grad_kv = combine_grads(grads, from_left, from_right, fast_rows, step_rows)

    first = jnp.where(even, mixed[:, :, :BLK], mixed[:, :, BLK:])
    second = jnp.where(even, mixed[:, :, BLK:], mixed[:, :, :BLK])
    project = lambda rows, full: jnp.einsum(
        "trk,tkn->rn", rows, full.reshape(tp, BLK, width), preferred_element_type=jnp.float32
    ).astype(jnp.bfloat16)
    first = project(first, mine)
    second = project(second, other)
    attended = jnp.where(even, first, second)
    grad_slow = jnp.where(even, second, first)

    summed, attended, grad_slow, grad_kv = lax.optimization_barrier((summed, attended, grad_slow, grad_kv))
    swapped = lax.ppermute(summed, "ctx", swap)
    cut = keep.shape[1]
    grad_q_weight = jnp.where(even, summed, swapped).astype(jnp.float32).reshape(q_weight.shape)
    blocked = jnp.where(even, swapped, summed).reshape(width // BLK, BLK // cut, cut, BLK).transpose(1, 2, 0, 3)
    grad_o_weight = blocked.astype(jnp.float32).reshape(o_weight.shape)
    return (attended, grad_slow, grad_q_weight, grad_o_weight, grad_kv)


def solution(mesh):
    in_specs = (
        P(("ctx", "tp"), None),
        P(None, "tp"),
        P("tp", None),
        P(None, "ctx", "tp"),
        P(),
        P(("ctx", "tp"), None),
    )
    out_specs = (
        P(("ctx", "tp"), None),
        P(("ctx", "tp"), None),
        P(None, "tp"),
        P("tp", None),
        P(None, "ctx", "tp"),
    )
    return jax.shard_map(on_device, mesh=mesh, in_specs=in_specs, out_specs=out_specs, check_vma=False)
```

```python
import functools

import jax
import jax.numpy as jnp
from jax import lax
from jax.experimental import pallas as pl
from jax.experimental.pallas import tpu as pltpu
from jax.sharding import PartitionSpec as P

BLK = 128
DH = 64
CHUNK = 512
MASKED = -1e30
VMEM_LIMIT = 58 * 1024 * 1024


def contract(a, b, dims):
    return lax.dot_general(a, b, (dims, ((), ())), preferred_element_type=jnp.float32)


def row_split(block):
    lane = lax.broadcasted_iota(jnp.int32, block.shape, 1)
    zero = jnp.zeros_like(block)
    return jnp.concatenate([jnp.where(lane < DH, block, zero), jnp.where(lane >= DH, block, zero)], axis=0)


def column_split(block):
    row = lax.broadcasted_iota(jnp.int32, block.shape, 0)
    zero = jnp.zeros_like(block)
    return jnp.concatenate([jnp.where(row < DH, block, zero), jnp.where(row >= DH, block, zero)], axis=1)


def column_join(wide):
    row = lax.broadcasted_iota(jnp.int32, (wide.shape[0], BLK), 0)
    return jnp.where(row < DH, wide[:, :BLK], wide[:, BLK:])


def pair_kernel(step_rows, window, scale, turn, moved, place, bias, lo_even, lo_odd, hi_even, hi_odd,
                q_weight, o_weight, left, own, right, *rest):
    pieces, rest = rest[: len(moved)], rest[len(moved) :]
    (grads, mixed, rows_out, weights, keys, values, probs, parts, grad_out, mixed_out, x_rows, g_rows,
     through, sems_in, sems_out, sems_row, sems_piece) = rest if turn == 0 else rest[4:]
    chunks, per = window // CHUNK, CHUNK // BLK
    pair = place[turn, 0]
    even = place[turn, 1] == 0
    rim, span = left.shape[1], own.shape[1]
    for block in range(bias.shape[0]):
        start = block * step_rows

        @pl.when(pair == block)
        def _():
            taken = 0
            for source, first in ((left, 0), (own, rim), (right, rim + span)):
                lo, hi = max(start, first), min(start + window, first + source.shape[1])
                if hi > lo:
                    for half, dest in enumerate((keys, values)):
                        pltpu.make_async_copy(
                            source.at[half, pl.ds(lo - first, hi - lo)], dest.at[pl.ds(taken, hi - lo)],
                            sems_in.at[half],
                        ).start()
                    taken += hi - lo

    copies = [pltpu.make_async_copy(own.at[half], dest, sems_in.at[half]) for half, dest in enumerate((keys, values))]
    half_rows = BLK // 2

    def fetch(lo, hi):
        return [
            pltpu.make_async_copy(
                source.at[pl.ds(part * half_rows, half_rows)], dest.at[pl.ds(side * half_rows, half_rows)],
                sems_row.at[2 + 2 * part + side],
            )
            for part, dest in enumerate((x_rows, g_rows))
            for side, source in enumerate((lo, hi))
        ]

    @pl.when(even)
    def _():
        for copy in fetch(lo_even, hi_even):
            copy.start()

    @pl.when(jnp.logical_not(even))
    def _():
        for copy in fetch(lo_odd, hi_odd):
            copy.start()

    arriving = [
        pltpu.make_async_copy(piece.at[pl.ds(first, BLK)], through.at[number], sems_piece.at[0, number])
        for number, (piece, (_, first)) in enumerate(zip(pieces, moved))
    ]
    for copy in arriving:
        copy.start()
    kept = []
    for copy in fetch(lo_even, hi_even):
        copy.wait()
    out_rows = pl.ds(pl.multiple_of(pair * BLK, BLK), BLK)
    for part, source in enumerate((x_rows, g_rows)):
        copy = pltpu.make_async_copy(source, rows_out.at[part, out_rows], sems_row.at[part])
        copy.start()
        kept.append(copy)

    q = (contract(x_rows[...], q_weight[...], ((1,), (0,))) * scale).astype(jnp.bfloat16)
    grad = contract(g_rows[...], o_weight[...], ((1,), (1,))).astype(jnp.bfloat16).astype(jnp.float32)
    q_t = column_split(q.T)
    query_rows = row_split(q)
    grad_t = grad.T
    wide, tall = column_split(grad_t), row_split(grad)

    at = lambda c: slice(c * CHUNK, (c + 1) * CHUNK)
    scores = lambda c: contract(keys[at(c), :], q_t, ((1,), (0,)))
    fold = lambda t, op: op(op(t.reshape(CHUNK // 8, 8, 2 * BLK), axis=0), axis=0, keepdims=True)

    def weigh(c, half):
        parts[c] = contract(values[at(c), :].T, half, ((1,), (0,)))

    copies[0].wait()
    tops, sums = [], []
    queue, held = [scores(0), scores(1)], None
    copies[1].wait()
    for c in range(chunks):
        s = queue.pop(0)
        if c + 2 < chunks:
            queue.append(scores(c + 2))
        s = jnp.concatenate([s[j * BLK : (j + 1) * BLK] + bias[pair, c * per + j] for j in range(per)], axis=0)
        top = fold(s, jnp.max)
        e = jnp.exp(s - top)
        tops.append(top)
        sums.append(fold(e, jnp.sum))
        half = e.astype(jnp.bfloat16)
        probs[at(c), :] = half
        if held is not None:
            weigh(c - 1, held)
        held = half
    weigh(chunks - 1, held)
    tops = jnp.concatenate(tops, axis=0)
    sums = jnp.concatenate(sums, axis=0)
    f = jnp.exp(tops - jnp.max(tops, axis=0, keepdims=True))
    f = f * (1.0 / jnp.sum(f * sums, axis=0, keepdims=True))
    out = parts[0] * f[:1]
    for c in range(1, chunks):
        out = out + parts[c] * f[c : c + 1]
    attn = column_join(out).T.astype(jnp.bfloat16)
    mixed_out[:, :BLK] = attn

    product = grad_t * attn.astype(jnp.float32).T
    delta = jnp.concatenate(
        [jnp.sum(product[:DH], axis=0, keepdims=True), jnp.sum(product[DH:], axis=0, keepdims=True)], axis=1
    )
    f_t = f.T
    homes = weights.shape[0]
    for number, (by, _) in enumerate(moved):
        arriving[number].wait()
        home = lax.rem(place[turn, 2] + (by + homes), homes)
        copy = pltpu.make_async_copy(through.at[number], weights.at[home], sems_piece.at[1, number])
        copy.start()
        kept.append(copy)
    lift = lambda c: contract(values[at(c), :], (wide * f[c : c + 1]).astype(jnp.bfloat16), ((1,), (0,)))
    total = jnp.zeros((BLK, 2 * BLK), jnp.float32)
    queue = [lift(0), lift(1)]
    sent = []
    for c in range(chunks):
        dp = queue.pop(0)
        if c + 2 < chunks:
            queue.append(lift(c + 2))
        e = probs[at(c), :]
        ds = (e.astype(jnp.float32) * (dp - delta * f[c : c + 1])).astype(jnp.bfloat16)
        total = total + contract(keys[at(c), :].T, ds, ((1,), (0,)))
        grad_out[0, at(c), :] = contract(ds, query_rows, ((1,), (0,))).astype(jnp.bfloat16)
        grad_out[1, at(c), :] = contract(
            e, (tall * f_t[:, c : c + 1]).astype(jnp.bfloat16), ((1,), (0,))
        ).astype(jnp.bfloat16)
        piece = pl.ds(c * CHUNK, CHUNK)
        copy = pltpu.make_async_copy(grad_out.at[:, piece], grads.at[pair, :, piece], sems_out.at[c])
        copy.start()
        sent.append(copy)
    mixed_out[:, BLK:] = (column_join(total) * scale).T.astype(jnp.bfloat16)
    copy = pltpu.make_async_copy(mixed_out, mixed.at[out_rows], sems_row.at[6])
    copy.start()
    for copy in sent + kept + [copy]:
        copy.wait()


def terms_kernel(flag, rows, mixed, keep, send):
    by_query = contract(mixed[:, BLK:], rows[0], ((0,), (0,))).T.astype(jnp.bfloat16)
    by_output = contract(mixed[:, :BLK], rows[1], ((0,), (0,))).astype(jnp.bfloat16)
    count, cut, _ = keep.shape
    groups = BLK // cut

    def store(q_out, o_out):
        for i in range(count):
            q_out[i] = by_query[i * cut : (i + 1) * cut, :]
            row, column = (i % groups) * cut, (i // groups) * BLK
            o_out[i] = by_output[row : row + cut, column : column + BLK]

    @pl.when(flag[0] == 0)
    def _():
        store(keep, send)

    @pl.when(flag[0] != 0)
    def _():
        store(send, keep)


def rim_kernel(step_rows, grads, left_out, right_out, far_l, near_l, far_r, near_r, sems):
    blocks, _, window, _ = grads.shape
    rim = left_out.shape[1]
    overlap = rim - step_rows
    copies = [
        pltpu.make_async_copy(grads.at[0, :, pl.ds(0, rim)], far_l, sems.at[0]),
        pltpu.make_async_copy(grads.at[1, :, pl.ds(0, overlap)], near_l, sems.at[1]),
        pltpu.make_async_copy(grads.at[blocks - 1, :, pl.ds(window - rim, rim)], far_r, sems.at[2]),
        pltpu.make_async_copy(grads.at[blocks - 2, :, pl.ds(window - overlap, overlap)], near_r, sems.at[3]),
    ]
    for copy in copies:
        copy.start()
    for copy in copies:
        copy.wait()
    add = lambda a, b: (a.astype(jnp.float32) + b.astype(jnp.float32)).astype(jnp.bfloat16)
    left_out[:, :step_rows, :] = far_l[:, :step_rows, :]
    left_out[:, step_rows:, :] = add(far_l[:, step_rows:, :], near_l[...])
    right_out[:, :overlap, :] = add(far_r[:, :overlap, :], near_r[...])
    right_out[:, overlap:, :] = far_r[:, overlap:, :]


def combine_kernel(step_rows, grads, from_left, from_right, out, held, result, sems, sems_out):
    blocks, _, window, _ = grads.shape
    rows, rim = out.shape[1], from_left.shape[1]
    plan = []
    slot = 0
    for first in range(0, rows, CHUNK):
        sources = []
        for block in range(blocks):
            local = first + rim - block * step_rows
            if 0 <= local < window:
                sources.append((grads.at[block, :, pl.ds(local, CHUNK)], slot))
                slot += 1
        if first < rim:
            sources.append((from_left.at[:, pl.ds(first, CHUNK)], slot))
            slot += 1
        if first >= rows - rim:
            sources.append((from_right.at[:, pl.ds(first - (rows - rim), CHUNK)], slot))
            slot += 1
        copies = [pltpu.make_async_copy(source, held.at[n], sems.at[n]) for source, n in sources]
        for copy in copies:
            copy.start()
        plan.append((first, sources, copies))
    sent = []
    for number, (first, sources, copies) in enumerate(plan):
        for copy in copies:
            copy.wait()
        part = held[sources[0][1]].astype(jnp.float32)
        for _, n in sources[1:]:
            part = part + held[n].astype(jnp.float32)
        result[:, first : first + CHUNK, :] = part.astype(jnp.bfloat16)
        piece = pl.ds(first, CHUNK)
        copy = pltpu.make_async_copy(result.at[:, piece], out.at[:, piece], sems_out.at[number])
        copy.start()
        sent.append(copy)
    for copy in sent:
        copy.wait()


ANYWHERE = pl.BlockSpec(memory_space=pl.ANY)
IN_VMEM = pl.BlockSpec(memory_space=pltpu.VMEM)
IN_SMEM = pl.BlockSpec(memory_space=pltpu.SMEM)


def params():
    return pltpu.CompilerParams(vmem_limit_bytes=VMEM_LIMIT)


def cost(flops, moved, exps=0):
    return pl.CostEstimate(flops=flops, bytes_accessed=moved, transcendentals=exps)


def pack_kernel(flag, x, g, o_weight, q_weight, kv, out, tail, head, sems):
    rows = x.shape[0]
    span, rim = kv.shape[1], tail.shape[1]
    copies = [
        pltpu.make_async_copy(kv.at[:, pl.ds(span - rim, rim)], tail, sems.at[0]),
        pltpu.make_async_copy(kv.at[:, pl.ds(0, rim)], head, sems.at[1]),
    ]
    for copy in copies:
        copy.start()
    out[:rows, :] = x[...]
    out[rows : 2 * rows, :] = g[...]

    @pl.when(flag[0] == 0)
    def _():
        out[2 * rows :, :] = o_weight[...]

    @pl.when(flag[0] != 0)
    def _():
        out[2 * rows :, :] = q_weight[...].T

    for copy in copies:
        copy.wait()


def pack(flag, x, g, o_weight, q_weight, kv, rim):
    edge = jax.ShapeDtypeStruct((2, rim, BLK), kv.dtype)
    return pl.pallas_call(
        pack_kernel,
        in_specs=[IN_SMEM] + [IN_VMEM] * 4 + [ANYWHERE],
        out_specs=[IN_VMEM] * 3,
        out_shape=[jax.ShapeDtypeStruct((2 * x.shape[0] + o_weight.shape[0], x.shape[1]), x.dtype), edge, edge],
        scratch_shapes=[pltpu.SemaphoreType.DMA((2,))],
        cost_estimate=cost(0, 4_000_000),
        name="pack",
    )(flag, x, g, o_weight, q_weight, kv)


def attention_pair(turn, place, bias, shards, moved, q_weight, o_weight, left, own, right, carried, blocks, homes,
                   step_rows, window):
    width = q_weight.shape[0]
    chunks = window // CHUNK
    shapes = [
        jax.ShapeDtypeStruct((blocks, 2, window, BLK), jnp.bfloat16),
        jax.ShapeDtypeStruct((blocks * BLK, 2 * BLK), jnp.bfloat16),
        jax.ShapeDtypeStruct((2, blocks * BLK, width), jnp.bfloat16),
        jax.ShapeDtypeStruct((homes, BLK, width), jnp.bfloat16),
    ]
    extra = () if carried is None else tuple(carried)
    pieces = [piece for piece, _, _ in moved]
    first_extra = 11 + len(pieces)
    bf = lambda *shape: pltpu.VMEM(shape, jnp.bfloat16)
    return pl.pallas_call(
        functools.partial(pair_kernel, step_rows, window, DH ** -0.5, turn, [m[1:] for m in moved]),
        in_specs=[IN_SMEM, IN_SMEM] + [ANYWHERE] * 4 + [IN_VMEM] * 2 + [ANYWHERE] * (3 + len(pieces) + len(extra)),
        out_specs=[ANYWHERE] * 4,
        out_shape=shapes,
        input_output_aliases={first_extra + i: i for i in range(len(extra))},
        scratch_shapes=[
            bf(window, BLK), bf(window, BLK),
            bf(window, 2 * BLK), pltpu.VMEM((chunks, BLK, 2 * BLK), jnp.float32),
            bf(2, window, BLK), bf(BLK, 2 * BLK), bf(BLK, width), bf(BLK, width), bf(len(pieces), BLK, width),
            pltpu.SemaphoreType.DMA((2,)), pltpu.SemaphoreType.DMA((chunks,)), pltpu.SemaphoreType.DMA((7,)),
            pltpu.SemaphoreType.DMA((2, len(pieces))),
        ],
        compiler_params=params(),
        cost_estimate=cost(4_000_000_000, 10_000_000, window * 2 * BLK),
        name="attention_pair",
    )(place, bias, *shards, q_weight, o_weight, left, own, right, *pieces, *extra)


def weight_terms(flag, rows, mixed, parts):
    half = jax.ShapeDtypeStruct((parts, rows.shape[2] // parts, BLK), jnp.bfloat16)
    return pl.pallas_call(
        terms_kernel,
        in_specs=[IN_SMEM] + [IN_VMEM] * 2,
        out_specs=[IN_VMEM] * 2,
        out_shape=[half, half],
        compiler_params=pltpu.CompilerParams(vmem_limit_bytes=24 * 1024 * 1024),
        cost_estimate=cost(1_000_000_000, 4_000_000),
        name="weight_terms",
    )(flag, rows, mixed)


def rim_grads(grads, rim, step_rows):
    bf = lambda rows: pltpu.VMEM((2, rows, BLK), jnp.bfloat16)
    edge = jax.ShapeDtypeStruct((2, rim, BLK), jnp.bfloat16)
    return pl.pallas_call(
        functools.partial(rim_kernel, step_rows),
        in_specs=[ANYWHERE],
        out_specs=[IN_VMEM] * 2,
        out_shape=[edge, edge],
        scratch_shapes=[bf(rim), bf(rim - step_rows), bf(rim), bf(rim - step_rows), pltpu.SemaphoreType.DMA((4,))],
        compiler_params=params(),
        cost_estimate=cost(1_000_000, 5_000_000),
        name="rim_grads",
    )(grads)


def combine_grads(grads, from_left, from_right, rows, step_rows):
    blocks, _, window, _ = grads.shape
    rim = from_left.shape[1]
    inside = sum(
        0 <= first + rim - block * step_rows < window for first in range(0, rows, CHUNK) for block in range(blocks)
    )
    slots = inside + 2 * (rim // CHUNK)
    return pl.pallas_call(
        functools.partial(combine_kernel, step_rows),
        in_specs=[ANYWHERE] * 3,
        out_specs=ANYWHERE,
        out_shape=jax.ShapeDtypeStruct((2, rows, BLK), jnp.bfloat16),
        scratch_shapes=[
            pltpu.VMEM((slots, 2, CHUNK, BLK), jnp.bfloat16),
            pltpu.VMEM((2, rows, BLK), jnp.bfloat16),
            pltpu.SemaphoreType.DMA((slots,)),
            pltpu.SemaphoreType.DMA((rows // CHUNK,)),
        ],
        compiler_params=params(),
        cost_estimate=cost(5_000_000, 10_000_000),
        name="combine_grads",
    )(grads, from_left, from_right)


def shifted(count, by):
    return [(i, (i + by) % count) for i in range(count)]


def band_bias(band_lists, base_block, query_blocks, half_step, reach_blocks):
    local = jnp.arange(query_blocks, dtype=jnp.int32)
    window_first = base_block + (2 * local + 1) * half_step - reach_blocks
    wanted = window_first[:, None] + jnp.arange(2 * reach_blocks, dtype=jnp.int32)[None, :]
    allowed = jnp.any(band_lists[:, :, None] == wanted[:, None, :], axis=1)
    return jnp.where(allowed, 0.0, MASKED).astype(jnp.float32)


def added(arrived):
    return jnp.sum(arrived.astype(jnp.float32), axis=0, keepdims=True).astype(jnp.bfloat16)


def exchange(parts, axis, groups=None):
    return lax.all_to_all(parts, axis, 0, 0, tiled=True, axis_index_groups=groups)


def on_device(slow_x, q_weight, o_weight, fast_kv, mask_lists, cotangent):
    own_rows, width = slow_x.shape
    tp = lax.axis_size("tp")
    ctx = lax.axis_size("ctx")
    total_rows = own_rows * tp
    query_blocks = total_rows // BLK
    fast_rows = fast_kv.shape[1]
    fast_blocks = fast_rows // BLK
    half_step = fast_blocks // (2 * query_blocks)
    reach_blocks = mask_lists.shape[1] // 2
    rim = (reach_blocks - half_step) * BLK
    window = 2 * reach_blocks * BLK
    step_rows = 2 * half_step * BLK

    ctx_index = lax.axis_index("ctx")
    flag = (ctx_index % 2).reshape(1).astype(jnp.int32)
    own, tail, head = pack(flag, slow_x, cotangent, o_weight, q_weight, fast_kv, rim)
    up = [(i, i + 1) for i in range(ctx - 1)]
    down = [(i + 1, i) for i in range(ctx - 1)]
    left = lax.ppermute(tail, "ctx", up)
    right = lax.ppermute(head, "ctx", down)

    even = ctx_index % 2 == 0
    band_lists = lax.dynamic_slice_in_dim(mask_lists, ctx_index * query_blocks, query_blocks, 0)
    bias = band_bias(band_lists, ctx_index * fast_blocks, query_blocks, half_step, reach_blocks)
    tp_index = lax.axis_index("tp")
    parity = tp_index % 2
    turn = 1 - 2 * parity
    middle = tp_index // 2
    moves = jnp.array([0, 0, 0, 2], jnp.int32) + jnp.array([0, -1, 1, 0], jnp.int32) * turn
    pairs = (middle + moves + query_blocks) % query_blocks
    spread = lambda value: jnp.broadcast_to(value, pairs.shape)
    place = jnp.stack([pairs, spread(parity), spread(tp_index)], axis=1).astype(jnp.int32)
    ahead, behind = shifted(tp, 1), shifted(tp, -1)
    shared = 2 * own_rows
    f, b = [own], [own]

    def pass_on(gate):
        back, front = f[-1], b[-1]
        if gate is not None:
            back, front, gate = lax.optimization_barrier((back, front, gate))
        if 2 * len(f) < tp:
            f.append(lax.ppermute(back, "tp", ahead))
            b.append(lax.ppermute(front, "tp", behind))
        else:
            f.append(lax.ppermute(back[:shared], "tp", ahead))
            b.append(lax.ppermute(front[shared:], "tp", behind))
        return gate

    picks = [
        lambda: ((own, f[1], b[1], own), [(own, 0, shared), (f[1], -1, shared), (b[1], 1, shared)]),
        lambda: ((f[2], b[1], f[1], b[2]), [(f[2], -2, shared), (b[2], 2, shared)]),
        lambda: ((b[2], f[3], b[3], f[2]), [(f[3], -3, shared), (b[3], 3, shared)]),
        lambda: ((f[4], b[3], f[3], f[4]), [(b[4], 4, 0)]),
    ]
    pass_on(None)
    pass_on(None)
    carried = None
    for number, pick in enumerate(picks):
        shards, moved = pick()
        carried = attention_pair(
            number, place, bias, shards, moved, q_weight, o_weight, left, fast_kv, right, carried, query_blocks, tp,
            step_rows, window,
        )
        if len(f) <= tp // 2:
            carried = (carried[0], pass_on(carried[1])) + tuple(carried[2:])
    grads, rows_mixed, rows_all, mine = carried

    mixed = exchange(rows_mixed.reshape(tp, own_rows, 2 * BLK), "tp")
    left_grads, right_grads = rim_grads(grads, rim, step_rows)
    rows_all, left_grads, right_grads = lax.optimization_barrier((rows_all, left_grads, right_grads))
    keep, send = weight_terms(flag, rows_all, rows_mixed, ctx)
    swap = [(i, i ^ 1) for i in range(ctx)]
    groups = [list(range(side, ctx, 2)) for side in range(2)]
    partner = lax.ppermute(send, "ctx", swap)
    keep, mixed = lax.optimization_barrier((keep, mixed))
    terms = (keep.astype(jnp.float32) + partner.astype(jnp.float32)).astype(jnp.bfloat16)
    terms = terms.reshape(ctx // 2, -1, BLK)
    arrived_terms = exchange(terms, "ctx", groups)
    from_right = lax.ppermute(left_grads, "ctx", down)
    from_left = lax.ppermute(right_grads, "ctx", up)
    other = lax.ppermute(mine, "ctx", [(i, i ^ 1) for i in range(ctx)])
    grad_kv = combine_grads(grads, from_left, from_right, fast_rows, step_rows)

    first = jnp.where(even, mixed[:, :, :BLK], mixed[:, :, BLK:])
    second = jnp.where(even, mixed[:, :, BLK:], mixed[:, :, :BLK])
    project = lambda rows, full: jnp.einsum(
        "trk,tkn->rn", rows, full.reshape(tp, BLK, width), preferred_element_type=jnp.float32
    ).astype(jnp.bfloat16)
    first = project(first, mine)
    second = project(second, other)
    attended = jnp.where(even, first, second)
    grad_slow = jnp.where(even, second, first)

    arrived_terms, attended, grad_slow = lax.optimization_barrier((arrived_terms, attended, grad_slow))
    own_terms = added(arrived_terms)
    summed = exchange(jnp.broadcast_to(own_terms, terms.shape), "ctx", groups)
    summed, grad_kv = lax.optimization_barrier((summed, grad_kv))
    swapped = lax.ppermute(summed, "ctx", swap)
    cut = keep.shape[1]
    grad_q_weight = jnp.where(even, summed, swapped).astype(jnp.float32).reshape(q_weight.shape)
    blocked = jnp.where(even, swapped, summed).reshape(width // BLK, BLK // cut, cut, BLK).transpose(1, 2, 0, 3)
    grad_o_weight = blocked.astype(jnp.float32).reshape(o_weight.shape)
    return (attended, grad_slow, grad_q_weight, grad_o_weight, grad_kv)


def solution(mesh):
    in_specs = (
        P(("ctx", "tp"), None),
        P(None, "tp"),
        P("tp", None),
        P(None, "ctx", "tp"),
        P(),
        P(("ctx", "tp"), None),
    )
    out_specs = (
        P(("ctx", "tp"), None),
        P(("ctx", "tp"), None),
        P(None, "tp"),
        P("tp", None),
        P(None, "ctx", "tp"),
    )
    return jax.shard_map(on_device, mesh=mesh, in_specs=in_specs, out_specs=out_specs, check_vma=False)
```
